256 devices in a mesh: dp: 32 (over x, z), tensor: 8 (over y, core).
Axes of the slice: x: 4, y: 4, z: 8, core: 2. Of those that a mesh axis runs over, the one named last changes fastest.
Arguments:
- grads: bfloat16 [32, 2, 512, 8192], P('dp', None, 'tensor'), may hold values from -6 to 6
- errors: bfloat16 [32, 2, 512, 8192], P('dp', None, 'tensor'), may hold values from -3 to 3
- q_init: bfloat16 [2, 8192, 32], replicated, may hold values from -6 to 6
Outputs:
- error_new: bfloat16 [32, 2, 512, 8192], P('dp', None, 'tensor')
- q_new: float32 [2, 8192, 32], replicated
- orthonormal: float32 [2, 512, 32], P(None, 'tensor')
The draws below stay inside these ranges and needn't reach their ends.
All inputs are finite; a program needn't handle non-finite values.
Results may differ from the reference program's by a relative error of at most 0.012.
Values sent between devices are 32-bit elements; how exact they have to be, the bound alone decides.
No kernel may reach another device: no remote copies, remote signals or barrier semaphores. Data moves between devices by JAX's collectives and lax.ppermute only.
A program may use at most 64 MiB of HBM per device.

```python
import jax
import jax.numpy as jnp
from jax import lax

COLS = 8192
R = 32
MATS = 2
ROWS = 512
N_DP = 32


def levels(key, dims, split, low, high):
    def one(position, blocks):
        draws = jax.random.uniform(jax.random.fold_in(jax.random.fold_in(key, 6), position), (blocks,), jnp.float32, low / len(split), high / len(split))
        return jnp.repeat(jnp.exp(draws), dims[position] // blocks).reshape((-1,) + (1,) * (len(dims) - position - 1))

    level = one(*split[0])
    for cut in split[1:]:
        level = level * one(*cut)
    return level


def noise(own_key, dims, deviation, reach, cuts=(), held_as=jnp.bfloat16):
    gain = levels(own_key, dims, cuts, -0.22, 0.18) if cuts else 1.0
    drawn = jax.random.normal(own_key, dims, jnp.float32) * deviation * gain
    return jnp.minimum(jnp.maximum(drawn, -reach), reach).astype(held_as)


def setup_inputs(seed: int = 0) -> dict:
    keys = jax.random.split(jax.random.key(seed), 4)
    return {
        "grads": noise(keys[0], (N_DP, MATS, ROWS, COLS), 1.0, 6.0, ((0, 32), (2, 8))),
        "errors": noise(keys[1], (N_DP, MATS, ROWS, COLS), 0.5, 3.0, ((0, 32), (2, 8))),
        "q_init": noise(keys[2], (MATS, COLS, R), 1.0, 6.0),
    }


def reference(grads, errors, q_init):

    def merge_one(replica):
        return (grads[replica].astype(jnp.float32) + errors[replica].astype(jnp.float32)).astype(jnp.bfloat16)

    def left_terms(total, replica):
        merged = merge_one(replica)
        terms = jnp.stack([jnp.dot(merged[matrix_index].astype(jnp.float32), q_init[matrix_index].astype(jnp.float32), preferred_element_type=jnp.float32) for matrix_index in range(MATS)])
        return (total + terms, None)
    summed, unused = lax.scan(left_terms, jnp.zeros((MATS, ROWS, R), jnp.float32), jnp.arange(N_DP, dtype=jnp.int32))
    columns = []
    for matrix_index in range(MATS):
        gram_matrix = jnp.dot(summed[matrix_index].T, summed[matrix_index], precision=lax.Precision.HIGHEST)
        factor = jnp.linalg.cholesky(gram_matrix)
        solved = lax.linalg.triangular_solve(factor, summed[matrix_index].T, left_side=True, lower=True)
        columns.append(solved.T)
    orthonormal = jnp.stack(columns)
    rounded_p = orthonormal.astype(jnp.bfloat16)

    def right_terms(total, replica):
        merged = merge_one(replica)
        terms = jnp.stack([jnp.dot(merged[matrix_index].T.astype(jnp.float32), rounded_p[matrix_index].astype(jnp.float32), preferred_element_type=jnp.float32) for matrix_index in range(MATS)])
        return (total + terms, None)
    q_total, unused = lax.scan(right_terms, jnp.zeros((MATS, COLS, R), jnp.float32), jnp.arange(N_DP, dtype=jnp.int32))
    q_new = q_total / N_DP
    rounded_q = q_new.astype(jnp.bfloat16)

    def new_error(replica):
        merged = merge_one(replica)
        approx = jnp.stack([jnp.dot(rounded_p[matrix_index].astype(jnp.float32), rounded_q[matrix_index].T.astype(jnp.float32), preferred_element_type=jnp.float32) for matrix_index in range(MATS)])
        return (merged.astype(jnp.float32) - approx).astype(jnp.bfloat16)
    error_new = lax.map(new_error, jnp.arange(N_DP, dtype=jnp.int32))
    return (error_new, q_new, orthonormal)
```

```python
import jax
import jax.numpy as jnp
from jax import lax
from jax.sharding import Mesh
from jax.sharding import PartitionSpec as P

NX, NZ, NY, NC = 4, 8, 4, 2
COLS, R, MATS, ROWS = 8192, 32, 2, 64
SPAN = COLS // (NX * NZ)


def split3(a):
    high = a.astype(jnp.bfloat16)
    rest = a - high.astype(jnp.float32)
    middle = rest.astype(jnp.bfloat16)
    low = (rest - middle.astype(jnp.float32)).astype(jnp.bfloat16)
    return high, middle, low


def swap(a):
    return lax.ppermute(a, "c", [(0, 1), (1, 0)])


def local(grads, errors, q_init):
    core = lax.axis_index("c")
    merged = (grads[0].astype(jnp.float32) + errors[0].astype(jnp.float32)).astype(jnp.bfloat16)
    terms = jnp.einsum("mck,mrc->kmr", q_init, merged, preferred_element_type=jnp.float32)
    terms = terms.reshape(R, MATS * ROWS)
    summed = jnp.sum(lax.all_gather(terms, "x"), axis=0)
    summed = jnp.sum(lax.all_gather(summed, "z"), axis=0)
    summed = summed.reshape(R, MATS, ROWS).transpose(1, 0, 2)

    pieces = jnp.concatenate(split3(summed), axis=1)
    products = jnp.einsum("mkr,mrc->mkc", pieces, merged, preferred_element_type=jnp.float32)
    products = products.reshape(MATS, 3, R, COLS)
    t_terms = products[:, 0] + (products[:, 1] + products[:, 2])

    gram = jnp.einsum("mkr,mlr->mkl", summed, summed, precision=lax.Precision.HIGHEST)
    gram = gram.reshape(MATS * R * R // 128, 128)
    gram = gram + swap(gram)
    gram = jnp.sum(lax.all_gather(gram, "y"), axis=0).reshape(MATS, R, R)
    factor = jnp.linalg.cholesky(gram)
    eye = jnp.broadcast_to(jnp.eye(R, dtype=jnp.float32), (MATS, R, R))
    inverse = lax.linalg.triangular_solve(factor, eye, left_side=True, lower=True)
    ortho = jnp.einsum("mkl,mlr->mrk", inverse, summed, precision=lax.Precision.HIGHEST)
    rounded_p = ortho.astype(jnp.bfloat16)

    mine = lax.dynamic_index_in_dim(t_terms, core, 0, keepdims=False)
    other = lax.dynamic_index_in_dim(t_terms, 1 - core, 0, keepdims=False)
    half = mine + swap(other)
    rows = jnp.sum(lax.all_to_all(half.reshape(NY, R // NY, COLS), "y", 0, 0), axis=0)
    blocks = rows.reshape(R // NY, NX * NZ, SPAN).transpose(1, 0, 2)
    own = jnp.sum(lax.all_to_all(blocks, ("x", "z"), 0, 0), axis=0)

    blocks = lax.all_to_all(jnp.broadcast_to(own[None], blocks.shape), ("x", "z"), 0, 0)
    rows = blocks.transpose(1, 0, 2).reshape(R // NY, COLS)
    half = lax.all_gather(rows, "y").reshape(R, COLS)
    inverse_mine = lax.dynamic_index_in_dim(inverse, core, 0, keepdims=False)
    q_mine = jnp.dot(inverse_mine, half, precision=lax.Precision.HIGHEST) / (NX * NZ)
    q_other = swap(q_mine)
    q_t = jnp.where(core == 0, jnp.stack([q_mine, q_other]), jnp.stack([q_other, q_mine]))
    rounded_q = q_t.astype(jnp.bfloat16)
    approx = jnp.einsum("mrk,mkc->mrc", rounded_p, rounded_q, preferred_element_type=jnp.float32)
    error_new = (merged.astype(jnp.float32) - approx).astype(jnp.bfloat16)
    return (error_new[None], q_t.transpose(0, 2, 1), ortho)


def solution(mesh):
    fine = Mesh(mesh.devices.reshape(NX, NZ, NY, NC), ("x", "z", "y", "c"))
    big = P(("x", "z"), None, ("y", "c"), None)
    return jax.shard_map(
        local,
        mesh=fine,
        in_specs=(big, big, P()),
        out_specs=(big, P(), P(None, ("y", "c"), None)),
        check_vma=False,
    )
```

```python
import jax
import jax.numpy as jnp
from jax import lax
from jax.experimental import pallas as pl
from jax.experimental.pallas import tpu as pltpu
from jax.sharding import Mesh
from jax.sharding import PartitionSpec as P

NX, NZ, NY, NC = 4, 8, 4, 2
COLS, R, MATS, ROWS = 8192, 32, 2, 64
WIDE = COLS // NX
SPAN = WIDE // NZ
HIGH = lax.Precision.HIGHEST
VMEM_LIMIT = 32 * 1024 * 1024


def swap(a):
    return lax.ppermute(a, "c", [(0, 1), (1, 0)])


def shifts(a, axis, size):
    return [lax.ppermute(a, axis, [(i, (i + s) % size) for i in range(size)]) for s in range(1, size)]


def copies_to_all(a, axes, count):
    return lax.all_to_all(jnp.broadcast_to(a[None], (count,) + a.shape), axes, 0, 0)


def merge(grads_ref, errors_ref):
    total = grads_ref[...].astype(jnp.float32) + errors_ref[...].astype(jnp.float32)
    return total.astype(jnp.bfloat16).reshape(ROWS, WIDE)


def right_terms(which_ref, summed_ref, grads_ref, errors_ref):
    both = summed_ref[...]
    value = jnp.where(which_ref[0] == 0, both[:, :ROWS], both[:, ROWS:])
    high = value.astype(jnp.bfloat16)
    rest = value - high.astype(jnp.float32)
    middle = rest.astype(jnp.bfloat16)
    low = (rest - middle.astype(jnp.float32)).astype(jnp.bfloat16)
    pieces = jnp.concatenate([high, middle, low], axis=0)
    products = jnp.dot(pieces, merge(grads_ref, errors_ref), preferred_element_type=jnp.float32)
    return products[:R] + (products[R : 2 * R] + products[2 * R :])


def first_half_kernel(which_ref, summed_ref, grads_ref, errors_ref, out_ref):
    out_ref[...] = right_terms(which_ref, summed_ref, grads_ref, errors_ref)


def second_half_kernel(which_ref, summed_ref, grads_ref, errors_ref, received_ref, out_ref):
    terms = right_terms(which_ref, summed_ref, grads_ref, errors_ref) + received_ref[...]
    out_ref[...] = terms.reshape(NY, 1, R // NY, WIDE)


MATRIX_BLOCK = pl.BlockSpec((1, 1, ROWS, WIDE), lambda i, which: (0, which[0], 0, i))
COLUMN_BLOCK = pl.BlockSpec((R, WIDE), lambda i, which: (0, i))
SPREAD_BLOCK = pl.BlockSpec((NY, 1, R // NY, WIDE), lambda i, which: (0, i, 0, 0))


def whole(*shape):
    return pl.BlockSpec(shape, lambda i, which: (0,) * len(shape))


def call(kernel, in_specs, out_specs, out_shape, flops, nbytes, aliases=None):
    return pl.pallas_call(
        kernel,
        grid_spec=pltpu.PrefetchScalarGridSpec(
            num_scalar_prefetch=1, grid=(NX,), in_specs=in_specs, out_specs=out_specs
        ),
        out_shape=out_shape,
        input_output_aliases=aliases or {},
        compiler_params=pltpu.CompilerParams(vmem_limit_bytes=VMEM_LIMIT),
        cost_estimate=pl.CostEstimate(flops=flops, bytes_accessed=nbytes, transcendentals=0),
    )


def right_first(which, summed, grads, errors):
    return call(
        first_half_kernel,
        [whole(R, MATS * ROWS), MATRIX_BLOCK, MATRIX_BLOCK],
        COLUMN_BLOCK,
        jax.ShapeDtypeStruct((R, COLS), jnp.float32),
        6 * ROWS * R * COLS,
        3 << 20,
    )(which, summed, grads, errors)


def right_second(which, summed, grads, errors, received):
    return call(
        second_half_kernel,
        [whole(R, MATS * ROWS), MATRIX_BLOCK, MATRIX_BLOCK, COLUMN_BLOCK],
        SPREAD_BLOCK,
        jax.ShapeDtypeStruct((NY, NX, R // NY, WIDE), jnp.float32),
        6 * ROWS * R * COLS,
        4 << 20,
    )(which, summed, grads, errors, received)


def factor_kernel(gram_ref, summed_ref, inverse_ref, ortho_ref):
    grams = gram_ref[0]
    for part in range(1, NY):
        grams = grams + gram_ref[part]
    row = lax.broadcasted_iota(jnp.int32, (R, 2 * R), 0)
    lane = lax.broadcasted_iota(jnp.int32, (R, 2 * R), 1)
    unit = (lane - R == row).astype(jnp.float32)[:, R:]
    states = [jnp.concatenate([grams[m * R : (m + 1) * R], unit], axis=1) for m in range(MATS)]
    for j in range(R):
        for m in range(MATS):
            x = states[m]
            pivot = x[j : j + 1]
            ratio = x[:, j : j + 1] * (1.0 / x[j : j + 1, j : j + 1])
            states[m] = x - jnp.where(row > j, ratio, 0.0) * pivot
    for m in range(MATS):
        x = states[m]
        diagonal = jnp.sum(jnp.where(row == lane, x, 0.0), axis=1, keepdims=True)
        inverse = x[:, R:] / jnp.sqrt(diagonal)
        inverse_ref[m] = inverse
        ortho_ref[m] = jnp.dot(
            inverse,
            summed_ref[:, m * ROWS : (m + 1) * ROWS],
            precision=HIGH,
            preferred_element_type=jnp.float32,
        )


def factors(grams, summed):
    return pl.pallas_call(
        factor_kernel,
        out_shape=(
            jax.ShapeDtypeStruct((MATS, R, R), jnp.float32),
            jax.ShapeDtypeStruct((MATS, R, ROWS), jnp.float32),
        ),
        cost_estimate=pl.CostEstimate(flops=1 << 20, bytes_accessed=12 << 20, transcendentals=0),
    )(grams, summed)


def finish_kernel(which_ref, inverse_ref, total_ref, out_ref):
    total = total_ref[...].reshape(R, WIDE)
    inverse = inverse_ref[0] * (1.0 / (NX * NZ))
    out_ref[...] = jnp.dot(inverse, total, precision=HIGH, preferred_element_type=jnp.float32)


def finish(which, inverse, total):
    return call(
        finish_kernel,
        [pl.BlockSpec((1, R, R), lambda i, which: (which[0], 0, 0)), SPREAD_BLOCK],
        COLUMN_BLOCK,
        jax.ShapeDtypeStruct((R, COLS), jnp.float32),
        2 * R * R * COLS,
        2 << 20,
    )(which, inverse, total)


def error_kernel(which_ref, ortho_ref, q_ref, grads_ref, errors_ref, *refs):
    error_ref, out_ref = refs[-2:]
    q = q_ref[...]
    approx = lax.dot_general(
        ortho_ref[0].astype(jnp.bfloat16),
        q.astype(jnp.bfloat16),
        (((0,), (0,)), ((), ())),
        preferred_element_type=jnp.float32,
    )
    error = merge(grads_ref, errors_ref).astype(jnp.float32) - approx
    error_ref[...] = error.astype(jnp.bfloat16).reshape(1, 1, ROWS, WIDE)
    out_ref[...] = q.reshape(1, R, WIDE)


def error_step(which, ortho, q, grads, errors, before=()):
    out_spec = pl.BlockSpec((1, R, WIDE), lambda i, which: (which[0], 0, i))
    untouched = pl.BlockSpec(memory_space=pl.ANY)
    ortho_spec = pl.BlockSpec((1, R, ROWS), lambda i, which: (which[0], 0, 0))
    return call(
        error_kernel,
        [ortho_spec, COLUMN_BLOCK, MATRIX_BLOCK, MATRIX_BLOCK] + [untouched] * len(before),
        [MATRIX_BLOCK, out_spec],
        (
            jax.ShapeDtypeStruct((1, MATS, ROWS, COLS), jnp.bfloat16),
            jax.ShapeDtypeStruct((MATS, R, COLS), jnp.float32),
        ),
        2 * ROWS * R * COLS,
        5 << 20,
        {5: 0, 6: 1} if before else None,
    )(which, ortho, q, grads, errors, *before)


def local(grads, errors, q_init):
    core = lax.axis_index("c").astype(jnp.int32)
    own = core.reshape(1)
    other = (1 - core).reshape(1)
    merged = (grads[0].astype(jnp.float32) + errors[0].astype(jnp.float32)).astype(jnp.bfloat16)
    terms = jnp.einsum("mck,mrc->kmr", q_init, merged, preferred_element_type=jnp.float32)
    terms = terms.reshape(R, MATS * ROWS)
    terms = jnp.sum(copies_to_all(terms, "x", NX), axis=0)
    summed = jnp.sum(copies_to_all(terms, "z", NZ), axis=0)

    split = summed.reshape(R, MATS, ROWS)
    gram = jnp.einsum("kmr,lmr->mkl", split, split, precision=HIGH).reshape(MATS * R, R)
    gram = gram + swap(gram)
    grams = jnp.stack([gram] + shifts(gram, "y", NY))

    received = swap(right_first(other, summed, grads, errors))
    half = right_second(own, summed, grads, errors, received)
    half = half.reshape(NY * NX, R // NY, WIDE)
    mine = jnp.sum(lax.all_to_all(half, ("y", "x"), 0, 0), axis=0)
    inverse, ortho = factors(grams, summed)
    mine = mine.reshape(R // NY, NZ, SPAN).transpose(1, 0, 2)
    mine = jnp.sum(lax.all_to_all(mine, "z", 0, 0), axis=0)

    total = copies_to_all(mine, "z", NZ).transpose(1, 0, 2).reshape(R // NY, WIDE)
    total = copies_to_all(total, ("y", "x"), NY * NX).reshape(NY, NX, R // NY, WIDE)
    q_own = finish(own, inverse, total)
    q_other = swap(q_own)
    first = error_step(own, ortho, q_own, grads, errors)
    error_new, q_t = error_step(other, ortho, q_other, grads, errors, first)
    return (error_new, q_t.transpose(0, 2, 1), ortho.transpose(0, 2, 1))


def solution(mesh):
    fine = Mesh(mesh.devices.reshape(NX, NZ, NY, NC), ("x", "z", "y", "c"))
    big = P(("x", "z"), None, ("y", "c"), None)
    return jax.shard_map(
        local,
        mesh=fine,
        in_specs=(big, big, P()),
        out_specs=(big, P(), P(None, ("y", "c"), None)),
        check_vma=False,
    )
```

```python
import jax
import jax.numpy as jnp
from jax import lax
from jax.experimental import pallas as pl
from jax.experimental.pallas import tpu as pltpu
from jax.sharding import Mesh
from jax.sharding import PartitionSpec as P

NX, NV, NW, NY, NC = 4, 4, 2, 4, 2
COLS, R, MATS, ROWS = 8192, 32, 2, 64
DP = NX * NV * NW
WIDE = COLS // NX
SPAN = WIDE // NW
K8 = R // NY
HIGH = lax.Precision.HIGHEST
VMEM_LIMIT = 32 * 1024 * 1024


def swap(a):
    return lax.ppermute(a, "c", [(0, 1), (1, 0)])


def shifts(a, axis, size):
    return [lax.ppermute(a, axis, [(i, (i + s) % size) for i in range(size)]) for s in range(1, size)]


def exchange(a, axes):
    return lax.all_to_all(a, axes, 0, 0)


def split3(value):
    high = value.astype(jnp.bfloat16)
    rest = value - high.astype(jnp.float32)
    middle = rest.astype(jnp.bfloat16)
    low = (rest - middle.astype(jnp.float32)).astype(jnp.bfloat16)
    return high, middle, low


def left_kernel(grads_ref, errors_ref, q_ref, merged_ref, copies_ref, total):
    step = pl.program_id(0)

    @pl.when(step == 0)
    def _():
        total[...] = jnp.zeros_like(total)

    for m in range(MATS):
        added = grads_ref[0, m].astype(jnp.float32) + errors_ref[0, m].astype(jnp.float32)
        merged = added.astype(jnp.bfloat16)
        merged_ref[m] = merged
        total[:, m * ROWS : (m + 1) * ROWS] += lax.dot_general(
            q_ref[m], merged, (((1,), (1,)), ((), ())), preferred_element_type=jnp.float32
        )

    @pl.when(step == NX - 1)
    def _():
        for copy in range(NX):
            copies_ref[copy] = total[...]


def left(grads, errors, q_t):
    block = pl.BlockSpec((1, MATS, ROWS, WIDE), lambda i: (0, 0, 0, i))
    return pl.pallas_call(
        left_kernel,
        grid=(NX,),
        in_specs=[block, block, pl.BlockSpec((MATS, R, WIDE), lambda i: (0, 0, i))],
        out_specs=[
            pl.BlockSpec((MATS, ROWS, WIDE), lambda i: (0, 0, i)),
            pl.BlockSpec((NX, R, MATS * ROWS), lambda i: (0, 0, 0)),
        ],
        out_shape=(
            jax.ShapeDtypeStruct((MATS, ROWS, COLS), jnp.bfloat16),
            jax.ShapeDtypeStruct((NX, R, MATS * ROWS), jnp.float32),
        ),
        scratch_shapes=[pltpu.VMEM((R, MATS * ROWS), jnp.float32)],
        compiler_params=pltpu.CompilerParams(vmem_limit_bytes=VMEM_LIMIT),
        cost_estimate=pl.CostEstimate(flops=1 << 27, bytes_accessed=7 << 20, transcendentals=0),
    )(grads, errors, q_t)


def sum_kernel(parts_ref, *refs):
    out_ref = refs[-1]
    total = parts_ref[0]
    for part in range(1, parts_ref.shape[0]):
        total = total + parts_ref[part]
    if len(out_ref.shape) == len(total.shape):
        out_ref[...] = total
    else:
        for copy in range(out_ref.shape[0]):
            out_ref[copy] = total


def sum_parts(parts, copies=None, after=()):
    shape = parts.shape[1:] if copies is None else (copies,) + parts.shape[1:]
    return pl.pallas_call(
        sum_kernel,
        in_specs=[pl.BlockSpec(memory_space=pltpu.VMEM)] + [pl.BlockSpec(memory_space=pl.ANY)] * len(after),
        out_specs=pl.BlockSpec(memory_space=pltpu.VMEM),
        out_shape=jax.ShapeDtypeStruct(shape, jnp.float32),
        compiler_params=pltpu.CompilerParams(vmem_limit_bytes=VMEM_LIMIT),
        cost_estimate=pl.CostEstimate(flops=1 << 18, bytes_accessed=1 << 20, transcendentals=0),
    )(parts, *after)


def right_terms(which_ref, summed_ref, merged_ref):
    both = summed_ref[...]
    value = jnp.where(which_ref[0] == 0, both[:, :ROWS], both[:, ROWS:])
    pieces = jnp.concatenate(split3(value), axis=0)
    products = jnp.dot(pieces, merged_ref[0], preferred_element_type=jnp.float32)
    return products[:R] + (products[R : 2 * R] + products[2 * R :])


def first_half_kernel(which_ref, summed_ref, merged_ref, gram_ref, out_ref):
    out_ref[...] = right_terms(which_ref, summed_ref, merged_ref)


def second_half_kernel(which_ref, summed_ref, merged_ref, received_ref, out_ref):
    terms = right_terms(which_ref, summed_ref, merged_ref) + received_ref[...]
    for w in range(NW):
        out_ref[0, w] = terms[:, w * SPAN : (w + 1) * SPAN].reshape(NY, K8, SPAN)


MATRIX_BLOCK = pl.BlockSpec((1, ROWS, WIDE), lambda i, which: (which[0], 0, i))
ERROR_BLOCK = pl.BlockSpec((1, 1, ROWS, WIDE), lambda i, which: (0, which[0], 0, i))
COLUMN_BLOCK = pl.BlockSpec((R, WIDE), lambda i, which: (0, i))
SPREAD_BLOCK = pl.BlockSpec((1, NW, NY, K8, SPAN), lambda i, which: (i, 0, 0, 0, 0))
UNTOUCHED = pl.BlockSpec(memory_space=pl.ANY)


def whole(*shape):
    return pl.BlockSpec(shape, lambda i, which: (0,) * len(shape))


def call(kernel, in_specs, out_specs, out_shape, flops, nbytes, aliases=None):
    return pl.pallas_call(
        kernel,
        grid_spec=pltpu.PrefetchScalarGridSpec(
            num_scalar_prefetch=1, grid=(NX,), in_specs=in_specs, out_specs=out_specs
        ),
        out_shape=out_shape,
        input_output_aliases=aliases or {},
        compiler_params=pltpu.CompilerParams(vmem_limit_bytes=VMEM_LIMIT),
        cost_estimate=pl.CostEstimate(flops=flops, bytes_accessed=nbytes, transcendentals=0),
    )


def right_first(which, summed, merged, gram):
    return call(
        first_half_kernel,
        [whole(R, MATS * ROWS), MATRIX_BLOCK, UNTOUCHED],
        COLUMN_BLOCK,
        jax.ShapeDtypeStruct((R, COLS), jnp.float32),
        6 * ROWS * R * COLS,
        2 << 20,
    )(which, summed, merged, gram)


def right_second(which, summed, merged, received):
    return call(
        second_half_kernel,
        [whole(R, MATS * ROWS), MATRIX_BLOCK, COLUMN_BLOCK],
        SPREAD_BLOCK,
        jax.ShapeDtypeStruct((NX, NW, NY, K8, SPAN), jnp.float32),
        6 * ROWS * R * COLS,
        3 << 20,
    )(which, summed, merged, received)


def factor_kernel(first_ref, second_ref, third_ref, fourth_ref, summed_ref, inverse_ref, ortho_ref):
    grams = (first_ref[...] + second_ref[...]) + (third_ref[...] + fourth_ref[...])
    row = lax.broadcasted_iota(jnp.int32, (R, 2 * R), 0)
    lane = lax.broadcasted_iota(jnp.int32, (R, 2 * R), 1)
    unit = (lane - R == row).astype(jnp.float32)[:, R:]
    states = [jnp.concatenate([grams[m * R : (m + 1) * R], unit], axis=1) for m in range(MATS)]
    for j in range(R):
        for m in range(MATS):
            x = states[m]
            pivot = x[j : j + 1]
            ratio = x[:, j : j + 1] * (1.0 / x[j : j + 1, j : j + 1])
            states[m] = x - jnp.where(row > j, ratio, 0.0) * pivot
    for m in range(MATS):
        x = states[m]
        diagonal = jnp.sum(jnp.where(row == lane, x, 0.0), axis=1, keepdims=True)
        inverse = x[:, R:] / jnp.sqrt(diagonal)
        inverse_ref[m] = inverse
        ortho_ref[m] = jnp.dot(
            inverse,
            summed_ref[:, m * ROWS : (m + 1) * ROWS],
            precision=HIGH,
            preferred_element_type=jnp.float32,
        )


def factors(grams, summed):
    return pl.pallas_call(
        factor_kernel,
        out_shape=(
            jax.ShapeDtypeStruct((MATS, R, R), jnp.float32),
            jax.ShapeDtypeStruct((MATS, R, ROWS), jnp.float32),
        ),
        cost_estimate=pl.CostEstimate(flops=1 << 20, bytes_accessed=12 << 20, transcendentals=0),
    )(*grams, summed)


def finish_kernel(which_ref, inverse_ref, total_ref, out_ref):
    a, b, c = split3(inverse_ref[0] * (1.0 / DP))
    left_pieces = jnp.concatenate([a, a, a, b, b, c], axis=1)
    for w in range(NW):
        high, middle, low = split3(total_ref[0, w].reshape(R, SPAN))
        right_pieces = jnp.concatenate([high, middle, low, high, middle, high], axis=0)
        out_ref[:, w * SPAN : (w + 1) * SPAN] = jnp.dot(
            left_pieces, right_pieces, preferred_element_type=jnp.float32
        )


def finish(which, inverse, total):
    return call(
        finish_kernel,
        [pl.BlockSpec((1, R, R), lambda i, which: (which[0], 0, 0)), SPREAD_BLOCK],
        COLUMN_BLOCK,
        jax.ShapeDtypeStruct((R, COLS), jnp.float32),
        2 * R * R * COLS,
        2 << 20,
    )(which, inverse, total)


def error_kernel(which_ref, ortho_ref, q_ref, merged_ref, *refs):
    error_ref, out_ref = refs[-2:]
    q = q_ref[...]
    approx = lax.dot_general(
        ortho_ref[0].astype(jnp.bfloat16),
        q.astype(jnp.bfloat16),
        (((0,), (0,)), ((), ())),
        preferred_element_type=jnp.float32,
    )
    error = merged_ref[0].astype(jnp.float32) - approx
    error_ref[...] = error.astype(jnp.bfloat16).reshape(1, 1, ROWS, WIDE)
    out_ref[...] = q.reshape(1, R, WIDE)


def error_step(which, ortho, q, merged, before=()):
    out_spec = pl.BlockSpec((1, R, WIDE), lambda i, which: (which[0], 0, i))
    ortho_spec = pl.BlockSpec((1, R, ROWS), lambda i, which: (which[0], 0, 0))
    return call(
        error_kernel,
        [ortho_spec, COLUMN_BLOCK, MATRIX_BLOCK] + [UNTOUCHED] * len(before),
        [ERROR_BLOCK, out_spec],
        (
            jax.ShapeDtypeStruct((1, MATS, ROWS, COLS), jnp.bfloat16),
            jax.ShapeDtypeStruct((MATS, R, COLS), jnp.float32),
        ),
        2 * ROWS * R * COLS,
        5 << 20,
        {4: 0, 5: 1} if before else None,
    )(which, ortho, q, merged, *before)


def local(grads, errors, q_init):
    core = lax.axis_index("c").astype(jnp.int32)
    own = core.reshape(1)
    other = (1 - core).reshape(1)
    merged, terms = left(grads, errors, q_init.transpose(0, 2, 1))
    terms = sum_parts(exchange(terms, "x"), NV * NW)
    summed = sum_parts(exchange(terms, ("v", "w")))

    split = summed.reshape(R, MATS, ROWS)
    gram = jnp.einsum("kmr,lmr->mkl", split, split, precision=HIGH).reshape(MATS * R, R)
    gram_pair = gram + swap(gram)
    grams = [gram_pair] + shifts(gram_pair, "y", NY)

    received = swap(right_first(other, summed, merged, gram))
    half = right_second(own, summed, merged, received)
    half = exchange(half.reshape(NX * NW * NY, K8, SPAN), ("x", "w", "y"))
    mine = sum_parts(half, NV, after=grams)
    inverse, ortho = factors(grams, summed)
    mine = sum_parts(exchange(mine, "v"), NX * NW * NY)

    total = exchange(mine, ("x", "w", "y")).reshape(NX, NW, NY, K8, SPAN)
    q_own = finish(own, inverse, total)
    q_other = swap(q_own)
    first = error_step(own, ortho, q_own, merged)
    error_new, q_t = error_step(other, ortho, q_other, merged, first)
    return (error_new, q_t.transpose(0, 2, 1), ortho.transpose(0, 2, 1))


def solution(mesh):
    fine = Mesh(mesh.devices.reshape(NX, NV, NW, NY, NC), ("x", "v", "w", "y", "c"))
    big = P(("x", "v", "w"), None, ("y", "c"), None)
    return jax.shard_map(
        local,
        mesh=fine,
        in_specs=(big, big, P()),
        out_specs=(big, P(), P(None, ("y", "c"), None)),
        check_vma=False,
    )
```

```python
import jax
import jax.numpy as jnp
from jax import lax
from jax.experimental import pallas as pl
from jax.experimental.pallas import tpu as pltpu
from jax.sharding import Mesh
from jax.sharding import PartitionSpec as P

NX, NV, NW, NY, NC = 4, 4, 2, 4, 2
COLS, R, MATS, ROWS = 8192, 32, 2, 64
DP = NX * NV * NW
GROUP = NX * NW * NY
BLOCK = COLS // GROUP
CHUNKS = 8
SPAN = COLS // CHUNKS
PER = GROUP // CHUNKS
AHEAD = 8
HIGH = lax.Precision.HIGHEST

IN_VMEM = pl.BlockSpec(memory_space=pltpu.VMEM)
IN_SMEM = pl.BlockSpec(memory_space=pltpu.SMEM)
IN_HBM = pl.BlockSpec(memory_space=pltpu.HBM)
ANYWHERE = pl.BlockSpec(memory_space=pl.ANY)
PARAMS = pltpu.CompilerParams(vmem_limit_bytes=16 * 1024 * 1024)


def cost(flops, nbytes):
    return pl.CostEstimate(flops=flops, bytes_accessed=nbytes, transcendentals=0)


def f32(*shape):
    return jax.ShapeDtypeStruct(shape, jnp.float32)


def vmem(*shape, dtype=jnp.float32):
    return pltpu.VMEM(shape, dtype)


def hbm(*shape, dtype=jnp.float32):
    return pltpu.HBM(shape, dtype)


def keep(a, space):
    return pltpu.with_memory_space_constraint(a, space)


def swap(a):
    return lax.ppermute(a, "c", [(0, 1), (1, 0)])


def shifts(a, axis, size):
    return [lax.ppermute(a, axis, [(i, (i + s) % size) for i in range(size)]) for s in range(1, size)]


def exchange(a, axes):
    return lax.all_to_all(a, axes, 0, 0)


def chunk(j):
    return pl.ds(j * SPAN, SPAN)


def split3(value):
    high = value.astype(jnp.bfloat16)
    rest = value - high.astype(jnp.float32)
    middle = rest.astype(jnp.bfloat16)
    low = (rest - middle.astype(jnp.float32)).astype(jnp.bfloat16)
    return high, middle, low


def start(pairs, sems):
    copies = [pltpu.make_async_copy(src, dst, sems.at[i]) for i, (src, dst) in enumerate(pairs)]
    for copy in copies:
        copy.start()
    return copies


def finish(copies):
    for copy in copies:
        copy.wait()


def left_kernel(
    core_ref, grads_hbm, errors_hbm, q_hbm, merged_ref, send_ref, mine_ref, theirs_ref, grads, errors, q, in_sems
):
    core = core_ref[0]
    def fetch(j):
        return start(
            [
                (grads_hbm.at[0, :, :, chunk(j)], grads.at[:, :, chunk(j)]),
                (errors_hbm.at[0, :, :, chunk(j)], errors.at[:, :, chunk(j)]),
                (q_hbm.at[:, :, chunk(j)], q.at[:, :, chunk(j)]),
            ],
            in_sems.at[j],
        )

    inward = [fetch(j) for j in range(AHEAD)]
    totals = [jnp.zeros((R, ROWS), jnp.float32) for _ in range(MATS)]
    for j in range(CHUNKS):
        finish(inward[j])
        if j + AHEAD < CHUNKS:
            inward.append(fetch(j + AHEAD))
        for m in range(MATS):
            total = grads[m, :, chunk(j)].astype(jnp.float32) + errors[m, :, chunk(j)].astype(jnp.float32)
            value = total.astype(jnp.bfloat16)
            merged_ref[m, :, chunk(j)] = value
            totals[m] += lax.dot_general(
                q[m, :, chunk(j)], value, (((1,), (1,)), ((), ())), preferred_element_type=jnp.float32
            )
        send_ref[:, chunk(j)] = merged_ref[1 - core, :, chunk(j)].astype(jnp.float32)
    mine_ref[...] = jnp.where(core == 0, totals[0], totals[1])
    theirs_ref[...] = jnp.where(core == 0, totals[1], totals[0])


def left(core, grads, errors, q_t):
    return pl.pallas_call(
        left_kernel,
        in_specs=[IN_SMEM, IN_HBM, IN_HBM, IN_HBM],
        out_specs=[IN_VMEM, IN_VMEM, IN_VMEM, IN_VMEM],
        out_shape=(
            vmem(MATS, ROWS, COLS, dtype=jnp.bfloat16),
            vmem(ROWS, COLS),
            vmem(R, ROWS),
            vmem(R, ROWS),
        ),
        scratch_shapes=[
            pltpu.VMEM((MATS, ROWS, COLS), jnp.bfloat16),
            pltpu.VMEM((MATS, ROWS, COLS), jnp.bfloat16),
            pltpu.VMEM((MATS, R, COLS), jnp.bfloat16),
            pltpu.SemaphoreType.DMA((CHUNKS, 3)),
        ],
        compiler_params=PARAMS,
        cost_estimate=cost(1 << 27, 9 << 20),
    )(core, keep(grads, pltpu.HBM), keep(errors, pltpu.HBM), keep(q_t, pltpu.HBM))


def added(parts_ref):
    value = parts_ref[0]
    for part in range(1, parts_ref.shape[0]):
        value = value + parts_ref[part]
    return value


def sum_kernel(parts_ref, *refs):
    out_ref = refs[-1]
    value = added(parts_ref)
    for copy in range(out_ref.shape[0]):
        out_ref[copy] = value


def sum_parts(parts, count, after=()):
    return pl.pallas_call(
        sum_kernel,
        in_specs=[IN_VMEM] + [IN_VMEM] * len(after),
        out_specs=IN_VMEM,
        out_shape=f32(count, *parts.shape[1:]),
        compiler_params=PARAMS,
        cost_estimate=cost(1 << 18, 2 << 20),
    )(parts, *[keep(a, pltpu.VMEM) for a in after])


def middle_kernel(parts_ref, inverse_ref, out_ref):
    total = added(parts_ref)
    q = jnp.dot(inverse_ref[...], total, precision=HIGH, preferred_element_type=jnp.float32) * (1.0 / DP)
    for copy in range(GROUP):
        out_ref[copy] = q


def middle(parts, inverse):
    return pl.pallas_call(
        middle_kernel,
        in_specs=[IN_VMEM, IN_VMEM],
        out_specs=IN_VMEM,
        out_shape=vmem(GROUP, R, BLOCK),
        compiler_params=PARAMS,
        cost_estimate=cost(1 << 20, 2 << 20),
    )(parts, inverse)


def right_kernel(core_ref, summed_ref, merged_ref, received_ref, out_ref, terms, out_sems):
    core = core_ref[0]
    pieces = jnp.concatenate(split3(summed_ref[...]), axis=0)
    outward = []
    for j in range(CHUNKS):
        both = jnp.concatenate(
            [merged_ref[core, :, chunk(j)], received_ref[:, chunk(j)].astype(jnp.bfloat16)], axis=0
        )
        products = jnp.dot(pieces, both, preferred_element_type=jnp.float32)
        value = products[:R] + (products[R : 2 * R] + products[2 * R :])
        for i in range(PER):
            terms[j * PER + i] = value[:, i * BLOCK : (i + 1) * BLOCK]
        outward += start([(terms.at[pl.ds(j * PER, PER)], out_ref.at[pl.ds(j * PER, PER)])], out_sems.at[j])
    finish(outward)


def right(core, summed, merged, received):
    return pl.pallas_call(
        right_kernel,
        in_specs=[IN_SMEM, IN_VMEM, IN_VMEM, IN_VMEM],
        out_specs=IN_HBM,
        out_shape=hbm(GROUP, R, BLOCK),
        scratch_shapes=[pltpu.VMEM((GROUP, R, BLOCK), jnp.float32), pltpu.SemaphoreType.DMA((CHUNKS, 1))],
        compiler_params=PARAMS,
        cost_estimate=cost(12 * ROWS * R * COLS, 4 << 20),
    )(core, summed, keep(merged, pltpu.VMEM), received)


def factor_kernel(first_ref, second_ref, third_ref, fourth_ref, summed_ref, inverse_ref, own_ref, theirs_ref):
    gram = (first_ref[...] + second_ref[...]) + (third_ref[...] + fourth_ref[...])
    row = lax.broadcasted_iota(jnp.int32, (R, 2 * R), 0)
    lane = lax.broadcasted_iota(jnp.int32, (R, 2 * R), 1)
    unit = (lane - R == row).astype(jnp.float32)[:, R:]
    x = jnp.concatenate([gram, unit], axis=1)
    for j in range(R):
        ratio = x[:, j : j + 1] * (1.0 / x[j : j + 1, j : j + 1])
        x = x - jnp.where(row > j, ratio, 0.0) * x[j : j + 1]
    diagonal = jnp.sum(jnp.where(row == lane, x, 0.0), axis=1, keepdims=True)
    inverse = x[:, R:] / jnp.sqrt(diagonal)
    inverse_ref[...] = inverse
    ortho = jnp.dot(inverse, summed_ref[...], precision=HIGH, preferred_element_type=jnp.float32)
    own_ref[...] = ortho[:, :ROWS]
    theirs_ref[...] = ortho[:, ROWS:]


def factors(grams, summed):
    return pl.pallas_call(
        factor_kernel,
        in_specs=[IN_VMEM] * (NY + 1),
        out_specs=[IN_VMEM] * 3,
        compiler_params=PARAMS,
        out_shape=(vmem(R, R), vmem(R, ROWS), vmem(R, ROWS)),
        cost_estimate=cost(1 << 20, 12 << 20),
    )(*[keep(a, pltpu.VMEM) for a in grams], keep(summed, pltpu.VMEM))


def tail_kernel(which_ref, ortho_ref, q_in, merged_ref, *refs):
    error_hbm, q_hbm, ortho_hbm, errors, q_new, ortho_sem, out_sems = refs[-7:]
    which = which_ref[0]
    outward = start([(ortho_ref, ortho_hbm.at[which])], ortho_sem)
    rounded_p = ortho_ref[...].astype(jnp.bfloat16)
    for j in range(CHUNKS):
        q = jnp.concatenate([q_in[j * PER + i] for i in range(PER)], axis=1)
        q_new[:, chunk(j)] = q
        approx = lax.dot_general(
            rounded_p, q.astype(jnp.bfloat16), (((0,), (0,)), ((), ())), preferred_element_type=jnp.float32
        )
        error = merged_ref[which, :, chunk(j)].astype(jnp.float32) - approx
        errors[:, chunk(j)] = error.astype(jnp.bfloat16)
        outward += start(
            [
                (q_new.at[:, chunk(j)], q_hbm.at[which, :, chunk(j)]),
                (errors.at[:, chunk(j)], error_hbm.at[0, which, :, chunk(j)]),
            ],
            out_sems.at[j],
        )
    finish(outward)


def tail(which, ortho, q, merged, before=()):
    return pl.pallas_call(
        tail_kernel,
        in_specs=[IN_SMEM, IN_VMEM, IN_VMEM, IN_VMEM] + [IN_HBM] * len(before),
        out_specs=[IN_HBM, IN_HBM, IN_HBM],
        out_shape=(hbm(1, MATS, ROWS, COLS, dtype=jnp.bfloat16), hbm(MATS, R, COLS), hbm(MATS, R, ROWS)),
        input_output_aliases={4: 0, 5: 1, 6: 2} if before else {},
        scratch_shapes=[
            pltpu.VMEM((ROWS, COLS), jnp.bfloat16),
            pltpu.VMEM((R, COLS), jnp.float32),
            pltpu.SemaphoreType.DMA((1,)),
            pltpu.SemaphoreType.DMA((CHUNKS, 2)),
        ],
        compiler_params=PARAMS,
        cost_estimate=cost(2 * ROWS * R * COLS, 4 << 20),
    )(which, keep(ortho, pltpu.VMEM), keep(q, pltpu.VMEM), keep(merged, pltpu.VMEM), *before)


def local(grads, errors, q_init):
    core = lax.axis_index("c").astype(jnp.int32)
    own = core.reshape(1)
    other = (1 - core).reshape(1)

    merged, send, mine, theirs = left(own, grads, errors, q_init.transpose(0, 2, 1))
    terms = jnp.concatenate([mine, swap(theirs)], axis=1)
    terms, send = lax.optimization_barrier((jnp.broadcast_to(terms[None], (NX,) + terms.shape), send))
    received = swap(send)
    terms = sum_parts(exchange(terms, "x"), NV * NW)
    summed = jnp.sum(exchange(terms, ("v", "w")), axis=0)

    gram = jnp.einsum("kr,lr->kl", summed, summed, precision=HIGH)
    grams = [gram] + shifts(gram, "y", NY)

    half = exchange(right(own, summed, merged, received), ("x", "w", "y"))
    part = sum_parts(half, NV, after=grams)
    inverse, ortho, ortho_theirs = factors(grams, summed)
    part = exchange(part, "v")

    q_own = exchange(middle(part, inverse), ("x", "w", "y"))
    q_other = swap(q_own)
    first = tail(own, ortho, q_own, merged)
    ortho_other, first = lax.optimization_barrier((swap(ortho_theirs), first))
    error_new, q_t, orthonormal = tail(other, ortho_other, q_other, merged, first)
    return (error_new, q_t.transpose(0, 2, 1), orthonormal.transpose(0, 2, 1))


def solution(mesh):
    fine = Mesh(mesh.devices.reshape(NX, NV, NW, NY, NC), ("x", "v", "w", "y", "c"))
    big = P(("x", "v", "w"), None, ("y", "c"), None)
    return jax.shard_map(
        local,
        mesh=fine,
        in_specs=(big, big, P()),
        out_specs=(big, P(), P(None, ("y", "c"), None)),
        check_vma=False,
    )
```

```python
import jax
import jax.numpy as jnp
from jax import lax
from jax.experimental import pallas as pl
from jax.experimental.pallas import tpu as pltpu
from jax.sharding import Mesh
from jax.sharding import PartitionSpec as P

NX, NV, NW, NY, NC = 4, 4, 2, 4, 2
COLS, R, MATS, ROWS = 8192, 32, 2, 64
DP = NX * NV * NW
GROUP = NX * NW * NY
BLOCK = COLS // GROUP
CHUNKS = 8
SPAN = COLS // CHUNKS
PER = GROUP // CHUNKS
AHEAD = 8
HIGH = lax.Precision.HIGHEST

IN_VMEM = pl.BlockSpec(memory_space=pltpu.VMEM)
IN_SMEM = pl.BlockSpec(memory_space=pltpu.SMEM)
IN_HBM = pl.BlockSpec(memory_space=pltpu.HBM)
ANYWHERE = pl.BlockSpec(memory_space=pl.ANY)
PARAMS = pltpu.CompilerParams(vmem_limit_bytes=16 * 1024 * 1024)


def cost(flops, nbytes):
    return pl.CostEstimate(flops=flops, bytes_accessed=nbytes, transcendentals=0)


def f32(*shape):
    return jax.ShapeDtypeStruct(shape, jnp.float32)


def vmem(*shape, dtype=jnp.float32):
    return pltpu.VMEM(shape, dtype)


def hbm(*shape, dtype=jnp.float32):
    return pltpu.HBM(shape, dtype)


def keep(a, space):
    return pltpu.with_memory_space_constraint(a, space)


def swap(a):
    return lax.ppermute(a, "c", [(0, 1), (1, 0)])


def shifts(a, axis, size):
    return [lax.ppermute(a, axis, [(i, (i + s) % size) for i in range(size)]) for s in range(1, size)]


def exchange(a, axes):
    return lax.all_to_all(a, axes, 0, 0)


def chunk(j):
    return pl.ds(j * SPAN, SPAN)


def split3(value):
    high = value.astype(jnp.bfloat16)
    rest = value - high.astype(jnp.float32)
    middle = rest.astype(jnp.bfloat16)
    low = (rest - middle.astype(jnp.float32)).astype(jnp.bfloat16)
    return high, middle, low


def start(pairs, sems):
    copies = [pltpu.make_async_copy(src, dst, sems.at[i]) for i, (src, dst) in enumerate(pairs)]
    for copy in copies:
        copy.start()
    return copies


def finish(copies):
    for copy in copies:
        copy.wait()


def left_kernel(
    core_ref, grads_hbm, errors_hbm, q_hbm, own_ref, other_ref, send_hbm, mine_ref, theirs_ref, grads, errors, q, send, in_sems, out_sems
):
    core = core_ref[0]
    inward = [
        start(
            [
                (grads_hbm.at[0, :, :, chunk(j)], grads.at[:, :, chunk(j)]),
                (errors_hbm.at[0, :, :, chunk(j)], errors.at[:, :, chunk(j)]),
                (q_hbm.at[:, :, chunk(j)], q.at[:, :, chunk(j)]),
            ],
            in_sems.at[j],
        )
        for j in range(CHUNKS)
    ]
    outward = []
    totals = [jnp.zeros((R, ROWS), jnp.float32) for _ in range(MATS)]
    for j in range(CHUNKS):
        finish(inward[j])
        for i, m in enumerate((core, 1 - core)):
            total = grads[m, :, chunk(j)].astype(jnp.float32) + errors[m, :, chunk(j)].astype(jnp.float32)
            merged = total.astype(jnp.bfloat16)
            totals[i] += lax.dot_general(
                q[m, :, chunk(j)], merged, (((1,), (1,)), ((), ())), preferred_element_type=jnp.float32
            )
            if i == 0:
                own_ref[:, chunk(j)] = merged
            else:
                other_ref[:, chunk(j)] = merged
                send[:, chunk(j)] = merged.astype(jnp.float32)
        outward += start([(send.at[:, chunk(j)], send_hbm.at[:, chunk(j)])], out_sems.at[j])
    mine_ref[...] = totals[0]
    theirs_ref[...] = totals[1]
    finish(outward)


def left(core, grads, errors, q_t):
    return pl.pallas_call(
        left_kernel,
        in_specs=[IN_SMEM, IN_HBM, IN_HBM, IN_HBM],
        out_specs=[IN_VMEM, IN_VMEM, IN_HBM, IN_VMEM, IN_VMEM],
        out_shape=(
            vmem(ROWS, COLS, dtype=jnp.bfloat16),
            vmem(ROWS, COLS, dtype=jnp.bfloat16),
            hbm(ROWS, COLS),
            vmem(R, ROWS),
            vmem(R, ROWS),
        ),
        scratch_shapes=[
            pltpu.VMEM((MATS, ROWS, COLS), jnp.bfloat16),
            pltpu.VMEM((MATS, ROWS, COLS), jnp.bfloat16),
            pltpu.VMEM((MATS, R, COLS), jnp.bfloat16),
            pltpu.VMEM((ROWS, COLS), jnp.float32),
            pltpu.SemaphoreType.DMA((CHUNKS, 3)),
            pltpu.SemaphoreType.DMA((CHUNKS, 1)),
        ],
        compiler_params=PARAMS,
        cost_estimate=cost(1 << 27, 9 << 20),
    )(core, keep(grads, pltpu.HBM), keep(errors, pltpu.HBM), keep(q_t, pltpu.HBM))


def added(parts_ref):
    value = parts_ref[0]
    for part in range(1, parts_ref.shape[0]):
        value = value + parts_ref[part]
    return value


def sum_kernel(parts_ref, *refs):
    out_ref = refs[-1]
    value = added(parts_ref)
    if len(out_ref.shape) == len(value.shape):
        out_ref[...] = value
    else:
        for copy in range(out_ref.shape[0]):
            out_ref[copy] = value


def sum_parts(parts, count=None, after=()):
    shape = parts.shape[1:] if count is None else (count,) + parts.shape[1:]
    return pl.pallas_call(
        sum_kernel,
        in_specs=[IN_VMEM] + [IN_VMEM] * len(after),
        out_specs=IN_VMEM,
        out_shape=f32(*shape),
        compiler_params=PARAMS,
        cost_estimate=cost(1 << 18, 2 << 20),
    )(parts, *[keep(a, pltpu.VMEM) for a in after])


def four_kernel(first_ref, second_ref, third_ref, fourth_ref, out_ref):
    value = (first_ref[...] + second_ref[...]) + (third_ref[...] + fourth_ref[...])
    for copy in range(out_ref.shape[0]):
        out_ref[copy] = value


def sum_four(parts, count):
    return pl.pallas_call(
        four_kernel,
        in_specs=[IN_VMEM] * 4,
        out_specs=IN_VMEM,
        out_shape=f32(count, *parts[0].shape),
        compiler_params=PARAMS,
        cost_estimate=cost(1 << 18, 2 << 20),
    )(*parts)


def middle_kernel(first_ref, second_ref, third_ref, fourth_ref, inverse_ref, out_ref):
    total = (first_ref[...] + second_ref[...]) + (third_ref[...] + fourth_ref[...])
    q = jnp.dot(inverse_ref[...], total, precision=HIGH, preferred_element_type=jnp.float32) * (1.0 / DP)
    for copy in range(GROUP):
        out_ref[copy] = q


def middle(parts, inverse):
    return pl.pallas_call(
        middle_kernel,
        in_specs=[IN_VMEM] * (NV + 1),
        out_specs=IN_VMEM,
        out_shape=vmem(GROUP, R, BLOCK),
        compiler_params=PARAMS,
        cost_estimate=cost(1 << 20, 2 << 20),
    )(*parts, inverse)


def right_kernel(summed_ref, merged_ref, received_ref, out_ref, terms, out_sems):
    pieces = jnp.concatenate(split3(summed_ref[...]), axis=0)
    outward = []
    for j in range(CHUNKS):
        both = jnp.concatenate(
            [merged_ref[:, chunk(j)], received_ref[:, chunk(j)].astype(jnp.bfloat16)], axis=0
        )
        products = jnp.dot(pieces, both, preferred_element_type=jnp.float32)
        value = products[:R] + (products[R : 2 * R] + products[2 * R :])
        for i in range(PER):
            terms[j * PER + i] = value[:, i * BLOCK : (i + 1) * BLOCK]
        outward += start([(terms.at[pl.ds(j * PER, PER)], out_ref.at[pl.ds(j * PER, PER)])], out_sems.at[j])
    finish(outward)


def right(summed, merged, received):
    return pl.pallas_call(
        right_kernel,
        in_specs=[IN_VMEM, IN_VMEM, IN_VMEM],
        out_specs=IN_HBM,
        out_shape=hbm(GROUP, R, BLOCK),
        scratch_shapes=[pltpu.VMEM((GROUP, R, BLOCK), jnp.float32), pltpu.SemaphoreType.DMA((CHUNKS, 1))],
        compiler_params=PARAMS,
        cost_estimate=cost(12 * ROWS * R * COLS, 4 << 20),
    )(summed, keep(merged, pltpu.VMEM), received)


def factor_kernel(first_ref, second_ref, third_ref, fourth_ref, summed_ref, inverse_ref, own_ref, theirs_ref):
    gram = (first_ref[...] + second_ref[...]) + (third_ref[...] + fourth_ref[...])
    row = lax.broadcasted_iota(jnp.int32, (R, 2 * R), 0)
    lane = lax.broadcasted_iota(jnp.int32, (R, 2 * R), 1)
    unit = (lane - R == row).astype(jnp.float32)[:, R:]
    x = jnp.concatenate([gram, unit], axis=1)
    for j in range(R):
        ratio = x[:, j : j + 1] * (1.0 / x[j : j + 1, j : j + 1])
        x = x - jnp.where(row > j, ratio, 0.0) * x[j : j + 1]
    diagonal = jnp.sum(jnp.where(row == lane, x, 0.0), axis=1, keepdims=True)
    inverse = x[:, R:] / jnp.sqrt(diagonal)
    inverse_ref[...] = inverse
    ortho = jnp.dot(inverse, summed_ref[...], precision=HIGH, preferred_element_type=jnp.float32)
    own_ref[...] = ortho[:, :ROWS]
    theirs_ref[...] = ortho[:, ROWS:]


def factors(grams, summed):
    return pl.pallas_call(
        factor_kernel,
        in_specs=[IN_VMEM] * (NY + 1),
        out_specs=[IN_VMEM] * 3,
        compiler_params=PARAMS,
        out_shape=(vmem(R, R), vmem(R, ROWS), vmem(R, ROWS)),
        cost_estimate=cost(1 << 20, 12 << 20),
    )(*[keep(a, pltpu.VMEM) for a in grams], keep(summed, pltpu.VMEM))


def tail_kernel(which_ref, ortho_ref, q_in, merged_ref, *refs):
    error_hbm, q_hbm, ortho_hbm, errors, q_new, ortho_sem, out_sems = refs[-7:]
    which = which_ref[0]
    outward = start([(ortho_ref, ortho_hbm.at[which])], ortho_sem)
    rounded_p = ortho_ref[...].astype(jnp.bfloat16)
    for j in range(CHUNKS):
        q = jnp.concatenate([q_in[j * PER + i] for i in range(PER)], axis=1)
        q_new[:, chunk(j)] = q
        approx = lax.dot_general(
            rounded_p, q.astype(jnp.bfloat16), (((0,), (0,)), ((), ())), preferred_element_type=jnp.float32
        )
        error = merged_ref[:, chunk(j)].astype(jnp.float32) - approx
        errors[:, chunk(j)] = error.astype(jnp.bfloat16)
        outward += start(
            [
                (q_new.at[:, chunk(j)], q_hbm.at[which, :, chunk(j)]),
                (errors.at[:, chunk(j)], error_hbm.at[0, which, :, chunk(j)]),
            ],
            out_sems.at[j],
        )
    finish(outward)


def tail(which, ortho, q, merged, before=()):
    return pl.pallas_call(
        tail_kernel,
        in_specs=[IN_SMEM, IN_VMEM, IN_VMEM, IN_VMEM] + [IN_HBM] * len(before),
        out_specs=[IN_HBM, IN_HBM, IN_HBM],
        out_shape=(hbm(1, MATS, ROWS, COLS, dtype=jnp.bfloat16), hbm(MATS, R, COLS), hbm(MATS, R, ROWS)),
        input_output_aliases={4: 0, 5: 1, 6: 2} if before else {},
        scratch_shapes=[
            pltpu.VMEM((ROWS, COLS), jnp.bfloat16),
            pltpu.VMEM((R, COLS), jnp.float32),
            pltpu.SemaphoreType.DMA((1,)),
            pltpu.SemaphoreType.DMA((CHUNKS, 2)),
        ],
        compiler_params=PARAMS,
        cost_estimate=cost(2 * ROWS * R * COLS, 4 << 20),
    )(which, keep(ortho, pltpu.VMEM), keep(q, pltpu.VMEM), keep(merged, pltpu.VMEM), *before)


def local(grads, errors, q_init):
    core = lax.axis_index("c").astype(jnp.int32)
    own = core.reshape(1)
    other = (1 - core).reshape(1)

    merged, merged_other, send, mine, theirs = left(own, grads, errors, q_init.transpose(0, 2, 1))
    terms = jnp.concatenate([mine, swap(theirs)], axis=1)
    terms, send = lax.optimization_barrier((terms, send))
    parts = [terms] + shifts(terms, "x", NX)
    received = swap(send)
    terms = sum_four(parts, NV * NW)
    summed = jnp.sum(exchange(terms, ("v", "w")), axis=0)

    gram = jnp.einsum("kr,lr->kl", summed, summed, precision=HIGH)
    grams = [gram] + shifts(gram, "y", NY)

    half = exchange(right(summed, merged, received), ("x", "w", "y"))
    part = sum_parts(half, after=grams)
    inverse, ortho, ortho_theirs = factors(grams, summed)
    parts = [part] + shifts(part, "v", NV)

    q_own = exchange(middle(parts, inverse), ("x", "w", "y"))
    q_other = swap(q_own)
    first = tail(own, ortho, q_own, merged)
    ortho_other, first = lax.optimization_barrier((swap(ortho_theirs), first))
    error_new, q_t, orthonormal = tail(other, ortho_other, q_other, merged_other, first)
    return (error_new, q_t.transpose(0, 2, 1), orthonormal.transpose(0, 2, 1))


def solution(mesh):
    fine = Mesh(mesh.devices.reshape(NX, NV, NW, NY, NC), ("x", "v", "w", "y", "c"))
    big = P(("x", "v", "w"), None, ("y", "c"), None)
    return jax.shard_map(
        local,
        mesh=fine,
        in_specs=(big, big, P()),
        out_specs=(big, P(), P(None, ("y", "c"), None)),
        check_vma=False,
    )
```

```python
import jax
import jax.numpy as jnp
from jax import lax
from jax.experimental import pallas as pl
from jax.experimental.pallas import tpu as pltpu
from jax.sharding import Mesh
from jax.sharding import PartitionSpec as P

NX, NV, NW, NY, NC = 4, 4, 2, 4, 2
COLS, R, MATS, ROWS = 8192, 32, 2, 64
DP = NX * NV * NW
GROUP = NX * NW * NY
BLOCK = COLS // GROUP
CHUNKS = 8
SPAN = COLS // CHUNKS
PER = GROUP // CHUNKS
AHEAD = 8
HIGH = lax.Precision.HIGHEST

IN_VMEM = pl.BlockSpec(memory_space=pltpu.VMEM)
IN_SMEM = pl.BlockSpec(memory_space=pltpu.SMEM)
IN_HBM = pl.BlockSpec(memory_space=pltpu.HBM)
ANYWHERE = pl.BlockSpec(memory_space=pl.ANY)
PARAMS = pltpu.CompilerParams(vmem_limit_bytes=16 * 1024 * 1024)


def cost(flops, nbytes):
    return pl.CostEstimate(flops=flops, bytes_accessed=nbytes, transcendentals=0)


def f32(*shape):
    return jax.ShapeDtypeStruct(shape, jnp.float32)


def vmem(*shape, dtype=jnp.float32):
    return pltpu.VMEM(shape, dtype)


def hbm(*shape, dtype=jnp.float32):
    return pltpu.HBM(shape, dtype)


def keep(a, space):
    return pltpu.with_memory_space_constraint(a, space)


def swap(a):
    return lax.ppermute(a, "c", [(0, 1), (1, 0)])


def shifts(a, axis, size):
    return [lax.ppermute(a, axis, [(i, (i + s) % size) for i in range(size)]) for s in (1, 3, 2)[: size - 1]]


def exchange(a, axes):
    return lax.all_to_all(a, axes, 0, 0)


def chunk(j):
    return pl.ds(j * SPAN, SPAN)


def split3(value):
    high = value.astype(jnp.bfloat16)
    rest = value - high.astype(jnp.float32)
    middle = rest.astype(jnp.bfloat16)
    low = (rest - middle.astype(jnp.float32)).astype(jnp.bfloat16)
    return high, middle, low


def start(pairs, sems):
    copies = [pltpu.make_async_copy(src, dst, sems.at[i]) for i, (src, dst) in enumerate(pairs)]
    for copy in copies:
        copy.start()
    return copies


def finish(copies):
    for copy in copies:
        copy.wait()


def left_kernel(
    core_ref, grads_hbm, errors_hbm, q_hbm, own_ref, other_ref, send_ref, mine_ref, theirs_ref, grads, errors, q, in_sems
):
    core = core_ref[0]
    inward = [
        start(
            [
                (grads_hbm.at[0, :, :, chunk(j)], grads.at[:, :, chunk(j)]),
                (errors_hbm.at[0, :, :, chunk(j)], errors.at[:, :, chunk(j)]),
                (q_hbm.at[:, :, chunk(j)], q.at[:, :, chunk(j)]),
            ],
            in_sems.at[j],
        )
        for j in range(CHUNKS)
    ]
    totals = [jnp.zeros((R, ROWS), jnp.float32) for _ in range(MATS)]
    for j in range(CHUNKS):
        finish(inward[j])
        for i, m in enumerate((core, 1 - core)):
            total = grads[m, :, chunk(j)].astype(jnp.float32) + errors[m, :, chunk(j)].astype(jnp.float32)
            merged = total.astype(jnp.bfloat16)
            totals[i] += lax.dot_general(
                q[m, :, chunk(j)], merged, (((1,), (1,)), ((), ())), preferred_element_type=jnp.float32
            )
            if i == 0:
                own_ref[:, chunk(j)] = merged
            else:
                other_ref[:, chunk(j)] = merged
                send_ref[:, chunk(j)] = merged.astype(jnp.float32)
    mine_ref[...] = totals[0]
    theirs_ref[...] = totals[1]


def left(core, grads, errors, q_t):
    return pl.pallas_call(
        left_kernel,
        in_specs=[IN_SMEM, IN_HBM, IN_HBM, IN_HBM],
        out_specs=[IN_VMEM] * 5,
        out_shape=(
            vmem(ROWS, COLS, dtype=jnp.bfloat16),
            vmem(ROWS, COLS, dtype=jnp.bfloat16),
            vmem(ROWS, COLS),
            vmem(R, ROWS),
            vmem(R, ROWS),
        ),
        scratch_shapes=[
            pltpu.VMEM((MATS, ROWS, COLS), jnp.bfloat16),
            pltpu.VMEM((MATS, ROWS, COLS), jnp.bfloat16),
            pltpu.VMEM((MATS, R, COLS), jnp.bfloat16),
            pltpu.SemaphoreType.DMA((CHUNKS, 3)),
        ],
        compiler_params=PARAMS,
        cost_estimate=cost(1 << 27, 9 << 20),
    )(core, keep(grads, pltpu.HBM), keep(errors, pltpu.HBM), keep(q_t, pltpu.HBM))


def added(parts_ref):
    value = parts_ref[0]
    for part in range(1, parts_ref.shape[0]):
        value = value + parts_ref[part]
    return value


def sum_kernel(parts_ref, *refs):
    out_ref = refs[-1]
    value = added(parts_ref)
    if len(out_ref.shape) == len(value.shape):
        out_ref[...] = value
    else:
        for copy in range(out_ref.shape[0]):
            out_ref[copy] = value


def sum_parts(parts, count=None, after=()):
    shape = parts.shape[1:] if count is None else (count,) + parts.shape[1:]
    return pl.pallas_call(
        sum_kernel,
        in_specs=[IN_VMEM] + [IN_VMEM] * len(after),
        out_specs=IN_VMEM,
        out_shape=f32(*shape),
        compiler_params=PARAMS,
        cost_estimate=cost(1 << 18, 2 << 20),
    )(parts, *[keep(a, pltpu.VMEM) for a in after])


def four_kernel(first_ref, second_ref, third_ref, fourth_ref, out_ref):
    value = (first_ref[...] + second_ref[...]) + (third_ref[...] + fourth_ref[...])
    out_ref[...] = value


def sum_four(parts):
    return pl.pallas_call(
        four_kernel,
        in_specs=[IN_VMEM] * 4,
        out_specs=IN_VMEM,
        out_shape=f32(*parts[0].shape),
        compiler_params=PARAMS,
        cost_estimate=cost(1 << 18, 2 << 20),
    )(*parts)


def middle_kernel(first_ref, second_ref, third_ref, fourth_ref, inverse_ref, out_ref):
    total = (first_ref[...] + second_ref[...]) + (third_ref[...] + fourth_ref[...])
    q = jnp.dot(inverse_ref[...], total, precision=HIGH, preferred_element_type=jnp.float32) * (1.0 / DP)
    for copy in range(GROUP):
        out_ref[copy] = q


def middle(parts, inverse):
    return pl.pallas_call(
        middle_kernel,
        in_specs=[IN_VMEM] * (NV + 1),
        out_specs=IN_VMEM,
        out_shape=vmem(GROUP, R, BLOCK),
        compiler_params=PARAMS,
        cost_estimate=cost(1 << 20, 2 << 20),
    )(*parts, inverse)


def right_kernel(summed_ref, merged_ref, received_ref, out_ref, terms, out_sems):
    pieces = jnp.concatenate(split3(summed_ref[...]), axis=0)
    outward = []
    for j in range(CHUNKS):
        both = jnp.concatenate(
            [merged_ref[:, chunk(j)], received_ref[:, chunk(j)].astype(jnp.bfloat16)], axis=0
        )
        products = jnp.dot(pieces, both, preferred_element_type=jnp.float32)
        value = products[:R] + (products[R : 2 * R] + products[2 * R :])
        for i in range(PER):
            terms[j * PER + i] = value[:, i * BLOCK : (i + 1) * BLOCK]
        outward += start([(terms.at[pl.ds(j * PER, PER)], out_ref.at[pl.ds(j * PER, PER)])], out_sems.at[j])
    finish(outward)


def right(summed, merged, received):
    return pl.pallas_call(
        right_kernel,
        in_specs=[IN_VMEM, IN_VMEM, IN_VMEM],
        out_specs=IN_HBM,
        out_shape=hbm(GROUP, R, BLOCK),
        scratch_shapes=[pltpu.VMEM((GROUP, R, BLOCK), jnp.float32), pltpu.SemaphoreType.DMA((CHUNKS, 1))],
        compiler_params=PARAMS,
        cost_estimate=cost(12 * ROWS * R * COLS, 4 << 20),
    )(summed, keep(merged, pltpu.VMEM), received)


def factor_kernel(first_ref, second_ref, third_ref, fourth_ref, summed_ref, inverse_ref, own_ref, theirs_ref):
    gram = (first_ref[...] + second_ref[...]) + (third_ref[...] + fourth_ref[...])
    row = lax.broadcasted_iota(jnp.int32, (R, 2 * R), 0)
    lane = lax.broadcasted_iota(jnp.int32, (R, 2 * R), 1)
    unit = (lane - R == row).astype(jnp.float32)[:, R:]
    x = jnp.concatenate([gram, unit], axis=1)
    for j in range(0, R, 2):
        row_a, row_b = x[j : j + 1], x[j + 1 : j + 2]
        column_a, column_b = x[:, j : j + 1], x[:, j + 1 : j + 2]
        pivot, between = row_a[:, j : j + 1], row_b[:, j : j + 1]
        inverse_a = 1.0 / pivot
        factor = between * inverse_a
        inverse_b = 1.0 / (row_b[:, j + 1 : j + 2] - factor * between)
        row_b = row_b - factor * row_a
        column_b = column_b - column_a * factor
        x = x - jnp.where(row > j, column_a * inverse_a, 0.0) * row_a
        x = x - jnp.where(row > j + 1, column_b * inverse_b, 0.0) * row_b
    diagonal = jnp.sum(jnp.where(row == lane, x, 0.0), axis=1, keepdims=True)
    inverse = x[:, R:] / jnp.sqrt(diagonal)
    inverse_ref[...] = inverse
    ortho = jnp.dot(inverse, summed_ref[...], precision=HIGH, preferred_element_type=jnp.float32)
    own_ref[...] = ortho[:, :ROWS]
    theirs_ref[...] = ortho[:, ROWS:]


def factors(grams, summed):
    return pl.pallas_call(
        factor_kernel,
        in_specs=[IN_VMEM] * (NY + 1),
        out_specs=[IN_VMEM] * 3,
        compiler_params=PARAMS,
        out_shape=(vmem(R, R), vmem(R, ROWS), vmem(R, ROWS)),
        cost_estimate=cost(1 << 20, 12 << 20),
    )(*[keep(a, pltpu.VMEM) for a in grams], keep(summed, pltpu.VMEM))


def spread_kernel(blocks_ref, out_ref):
    for i in range(GROUP):
        out_ref[:, i * BLOCK : (i + 1) * BLOCK] = blocks_ref[i]


def spread(blocks):
    return pl.pallas_call(
        spread_kernel,
        in_specs=[IN_VMEM],
        out_specs=IN_VMEM,
        out_shape=vmem(R, COLS),
        compiler_params=PARAMS,
        cost_estimate=cost(0, 2 << 20),
    )(blocks)


def tail_kernel(which_ref, ortho_ref, q_ref, merged_ref, *refs):
    error_hbm, q_hbm, ortho_hbm, errors, sems, out_sems = refs[-6:]
    which = which_ref[0]
    outward = start([(q_ref, q_hbm.at[which]), (ortho_ref, ortho_hbm.at[which])], sems)
    rounded_p = ortho_ref[...].astype(jnp.bfloat16)
    for j in range(CHUNKS):
        approx = lax.dot_general(
            rounded_p,
            q_ref[:, chunk(j)].astype(jnp.bfloat16),
            (((0,), (0,)), ((), ())),
            preferred_element_type=jnp.float32,
        )
        error = merged_ref[:, chunk(j)].astype(jnp.float32) - approx
        errors[:, chunk(j)] = error.astype(jnp.bfloat16)
        outward += start([(errors.at[:, chunk(j)], error_hbm.at[0, which, :, chunk(j)])], out_sems.at[j])
    finish(outward)


def tail(which, ortho, q, merged, before=()):
    return pl.pallas_call(
        tail_kernel,
        in_specs=[IN_SMEM, IN_VMEM, IN_VMEM, IN_VMEM] + [IN_HBM] * len(before),
        out_specs=[IN_HBM, IN_HBM, IN_HBM],
        out_shape=(hbm(1, MATS, ROWS, COLS, dtype=jnp.bfloat16), hbm(MATS, R, COLS), hbm(MATS, R, ROWS)),
        input_output_aliases={4: 0, 5: 1, 6: 2} if before else {},
        scratch_shapes=[
            pltpu.VMEM((ROWS, COLS), jnp.bfloat16),
            pltpu.SemaphoreType.DMA((2,)),
            pltpu.SemaphoreType.DMA((CHUNKS, 1)),
        ],
        compiler_params=PARAMS,
        cost_estimate=cost(2 * ROWS * R * COLS, 4 << 20),
    )(which, keep(ortho, pltpu.VMEM), keep(q, pltpu.VMEM), keep(merged, pltpu.VMEM), *before)


def local(grads, errors, q_init):
    core = lax.axis_index("c").astype(jnp.int32)
    own = core.reshape(1)
    other = (1 - core).reshape(1)

    merged, merged_other, send, mine, theirs = left(own, grads, errors, q_init.transpose(0, 2, 1))
    terms = jnp.concatenate([mine, swap(theirs)], axis=1)
    terms, send = lax.optimization_barrier((terms, send))
    parts = [terms] + shifts(terms, "x", NX)
    received = swap(send)
    terms = sum_four(parts)
    terms = terms + shifts(terms, "w", NW)[0]
    summed = sum_four([terms] + shifts(terms, "v", NV))

    gram = jnp.einsum("kr,lr->kl", summed, summed, precision=HIGH)
    grams = [gram] + shifts(gram, "y", NY)

    half = exchange(right(summed, merged, received), ("x", "w", "y"))
    part = sum_parts(half, after=grams)
    inverse, ortho, ortho_theirs = factors(grams, summed)
    parts = [part] + shifts(part, "v", NV)

    q_own = spread(exchange(middle(parts, inverse), ("x", "w", "y")))
    q_other = swap(q_own)
    first = tail(own, ortho, q_own, merged)
    ortho_other, first = lax.optimization_barrier((swap(ortho_theirs), first))
    error_new, q_t, orthonormal = tail(other, ortho_other, q_other, merged_other, first)
    return (error_new, q_t.transpose(0, 2, 1), orthonormal.transpose(0, 2, 1))


def solution(mesh):
    fine = Mesh(mesh.devices.reshape(NX, NV, NW, NY, NC), ("x", "v", "w", "y", "c"))
    big = P(("x", "v", "w"), None, ("y", "c"), None)
    return jax.shard_map(
        local,
        mesh=fine,
        in_specs=(big, big, P()),
        out_specs=(big, P(), P(None, ("y", "c"), None)),
        check_vma=False,
    )
```

```python
import functools

import jax
import jax.numpy as jnp
from jax import lax
from jax.experimental import pallas as pl
from jax.experimental.pallas import tpu as pltpu
from jax.sharding import Mesh
from jax.sharding import PartitionSpec as P

NX, NV, NW, NY, NC = 4, 4, 2, 4, 2
COLS, R, MATS, ROWS = 8192, 32, 2, 64
DP = NX * NV * NW
GROUP = NX * NW * NY
BLOCK = COLS // GROUP
CHUNKS = 8
SPAN = COLS // CHUNKS
PER = GROUP // CHUNKS
AHEAD = 8
HIGH = lax.Precision.HIGHEST

IN_VMEM = pl.BlockSpec(memory_space=pltpu.VMEM)
IN_SMEM = pl.BlockSpec(memory_space=pltpu.SMEM)
IN_HBM = pl.BlockSpec(memory_space=pltpu.HBM)
ANYWHERE = pl.BlockSpec(memory_space=pl.ANY)
PARAMS = pltpu.CompilerParams(vmem_limit_bytes=16 * 1024 * 1024)


def cost(flops, nbytes):
    return pl.CostEstimate(flops=flops, bytes_accessed=nbytes, transcendentals=0)


def f32(*shape):
    return jax.ShapeDtypeStruct(shape, jnp.float32)


def vmem(*shape, dtype=jnp.float32):
    return pltpu.VMEM(shape, dtype)


def hbm(*shape, dtype=jnp.float32):
    return pltpu.HBM(shape, dtype)


def keep(a, space):
    return pltpu.with_memory_space_constraint(a, space)


def swap(a):
    return lax.ppermute(a, "c", [(0, 1), (1, 0)])


def shifts(a, axis, size):
    return [lax.ppermute(a, axis, [(i, (i + s) % size) for i in range(size)]) for s in (1, 3, 2)[: size - 1]]


def exchange(a, axes):
    return lax.all_to_all(a, axes, 0, 0)


def chunk(j):
    return pl.ds(j * SPAN, SPAN)


def split3(value):
    high = value.astype(jnp.bfloat16)
    rest = value - high.astype(jnp.float32)
    middle = rest.astype(jnp.bfloat16)
    low = (rest - middle.astype(jnp.float32)).astype(jnp.bfloat16)
    return high, middle, low


def start(pairs, sems):
    copies = [pltpu.make_async_copy(src, dst, sems.at[i]) for i, (src, dst) in enumerate(pairs)]
    for copy in copies:
        copy.start()
    return copies


def finish(copies):
    for copy in copies:
        copy.wait()


def left_kernel(
    core_ref, grads_hbm, errors_hbm, q_hbm, own_ref, other_ref, send_ref, mine_ref, theirs_ref, grads, errors, q, in_sems
):
    core = core_ref[0]
    inward = [
        start(
            [
                (grads_hbm.at[0, :, :, chunk(j)], grads.at[:, :, chunk(j)]),
                (errors_hbm.at[0, :, :, chunk(j)], errors.at[:, :, chunk(j)]),
                (q_hbm.at[:, :, chunk(j)], q.at[:, :, chunk(j)]),
            ],
            in_sems.at[j],
        )
        for j in range(CHUNKS)
    ]
    totals = [jnp.zeros((R, ROWS), jnp.float32) for _ in range(MATS)]
    for j in range(CHUNKS):
        finish(inward[j])
        for i, m in enumerate((core, 1 - core)):
            total = grads[m, :, chunk(j)].astype(jnp.float32) + errors[m, :, chunk(j)].astype(jnp.float32)
            merged = total.astype(jnp.bfloat16)
            totals[i] += lax.dot_general(
                q[m, :, chunk(j)], merged, (((1,), (1,)), ((), ())), preferred_element_type=jnp.float32
            )
            if i == 0:
                own_ref[:, chunk(j)] = merged
            else:
                other_ref[:, chunk(j)] = merged
                send_ref[:, chunk(j)] = merged.astype(jnp.float32)
    mine_ref[...] = totals[0]
    theirs_ref[...] = totals[1]


def left(core, grads, errors, q_t):
    return pl.pallas_call(
        left_kernel,
        in_specs=[IN_SMEM, IN_HBM, IN_HBM, IN_HBM],
        out_specs=[IN_VMEM] * 5,
        out_shape=(
            vmem(ROWS, COLS, dtype=jnp.bfloat16),
            vmem(ROWS, COLS, dtype=jnp.bfloat16),
            vmem(ROWS, COLS),
            vmem(R, ROWS),
            vmem(R, ROWS),
        ),
        scratch_shapes=[
            pltpu.VMEM((MATS, ROWS, COLS), jnp.bfloat16),
            pltpu.VMEM((MATS, ROWS, COLS), jnp.bfloat16),
            pltpu.VMEM((MATS, R, COLS), jnp.bfloat16),
            pltpu.SemaphoreType.DMA((CHUNKS, 3)),
        ],
        compiler_params=PARAMS,
        cost_estimate=cost(1 << 27, 9 << 20),
    )(core, keep(grads, pltpu.HBM), keep(errors, pltpu.HBM), keep(q_t, pltpu.HBM))


def added(parts_ref):
    value = parts_ref[0]
    for part in range(1, parts_ref.shape[0]):
        value = value + parts_ref[part]
    return value


def sum_kernel(parts_ref, *refs):
    out_ref = refs[-1]
    value = added(parts_ref)
    if len(out_ref.shape) == len(value.shape):
        out_ref[...] = value
    else:
        for copy in range(out_ref.shape[0]):
            out_ref[copy] = value


def sum_parts(parts, count=None, after=()):
    shape = parts.shape[1:] if count is None else (count,) + parts.shape[1:]
    return pl.pallas_call(
        sum_kernel,
        in_specs=[IN_VMEM] + [IN_VMEM] * len(after),
        out_specs=IN_VMEM,
        out_shape=f32(*shape),
        compiler_params=PARAMS,
        cost_estimate=cost(1 << 18, 2 << 20),
    )(parts, *[keep(a, pltpu.VMEM) for a in after])


def four_kernel(first_ref, second_ref, third_ref, fourth_ref, out_ref):
    value = (first_ref[...] + second_ref[...]) + (third_ref[...] + fourth_ref[...])
    out_ref[...] = value


def sum_four(parts):
    return pl.pallas_call(
        four_kernel,
        in_specs=[IN_VMEM] * 4,
        out_specs=IN_VMEM,
        out_shape=f32(*parts[0].shape),
        compiler_params=PARAMS,
        cost_estimate=cost(1 << 18, 2 << 20),
    )(*parts)


def middle_kernel(first_ref, second_ref, third_ref, fourth_ref, inverse_ref, out_ref):
    total = (first_ref[...] + second_ref[...]) + (third_ref[...] + fourth_ref[...])
    q = jnp.dot(inverse_ref[...], total, precision=HIGH, preferred_element_type=jnp.float32) * (1.0 / DP)
    for copy in range(GROUP):
        out_ref[copy] = q


def middle(parts, inverse):
    return pl.pallas_call(
        middle_kernel,
        in_specs=[IN_VMEM] * (NV + 1),
        out_specs=IN_VMEM,
        out_shape=vmem(GROUP, R, BLOCK),
        compiler_params=PARAMS,
        cost_estimate=cost(1 << 20, 2 << 20),
    )(*parts, inverse)


def right_kernel(summed_ref, merged_ref, received_ref, out_ref, terms, out_sems):
    pieces = jnp.concatenate(split3(summed_ref[...]), axis=0)
    outward = []
    for j in range(CHUNKS):
        both = jnp.concatenate(
            [merged_ref[:, chunk(j)], received_ref[:, chunk(j)].astype(jnp.bfloat16)], axis=0
        )
        products = jnp.dot(pieces, both, preferred_element_type=jnp.float32)
        value = products[:R] + (products[R : 2 * R] + products[2 * R :])
        for i in range(PER):
            terms[j * PER + i] = value[:, i * BLOCK : (i + 1) * BLOCK]
        outward += start([(terms.at[pl.ds(j * PER, PER)], out_ref.at[pl.ds(j * PER, PER)])], out_sems.at[j])
    finish(outward)


def right(summed, merged, received):
    return pl.pallas_call(
        right_kernel,
        in_specs=[IN_VMEM, IN_VMEM, IN_VMEM],
        out_specs=IN_HBM,
        out_shape=hbm(GROUP, R, BLOCK),
        scratch_shapes=[pltpu.VMEM((GROUP, R, BLOCK), jnp.float32), pltpu.SemaphoreType.DMA((CHUNKS, 1))],
        compiler_params=PARAMS,
        cost_estimate=cost(12 * ROWS * R * COLS, 4 << 20),
    )(summed, keep(merged, pltpu.VMEM), received)


def factor_kernel(first_ref, second_ref, third_ref, fourth_ref, summed_ref, inverse_ref, own_ref, theirs_ref):
    gram = (first_ref[...] + second_ref[...]) + (third_ref[...] + fourth_ref[...])
    row = lax.broadcasted_iota(jnp.int32, (R, 2 * R), 0)
    lane = lax.broadcasted_iota(jnp.int32, (R, 2 * R), 1)
    unit = (lane - R == row).astype(jnp.float32)[:, R:]
    x = jnp.concatenate([gram, unit], axis=1)
    for j in range(0, R, 2):
        row_a, row_b = x[j : j + 1], x[j + 1 : j + 2]
        column_a, column_b = x[:, j : j + 1], x[:, j + 1 : j + 2]
        pivot, between = row_a[:, j : j + 1], row_b[:, j : j + 1]
        inverse_a = 1.0 / pivot
        factor = between * inverse_a
        inverse_b = 1.0 / (row_b[:, j + 1 : j + 2] - factor * between)
        row_b = row_b - factor * row_a
        column_b = column_b - column_a * factor
        x = x - jnp.where(row > j, column_a * inverse_a, 0.0) * row_a
        x = x - jnp.where(row > j + 1, column_b * inverse_b, 0.0) * row_b
    diagonal = jnp.sum(jnp.where(row == lane, x, 0.0), axis=1, keepdims=True)
    inverse = x[:, R:] / jnp.sqrt(diagonal)
    inverse_ref[...] = inverse
    ortho = jnp.dot(inverse, summed_ref[...], precision=HIGH, preferred_element_type=jnp.float32)
    own_ref[...] = ortho[:, :ROWS]
    theirs_ref[...] = ortho[:, ROWS:]


def factors(grams, summed):
    return pl.pallas_call(
        factor_kernel,
        in_specs=[IN_VMEM] * (NY + 1),
        out_specs=[IN_VMEM] * 3,
        compiler_params=PARAMS,
        out_shape=(vmem(R, R), vmem(R, ROWS), vmem(R, ROWS)),
        cost_estimate=cost(1 << 20, 12 << 20),
    )(*[keep(a, pltpu.VMEM) for a in grams], keep(summed, pltpu.VMEM))


def spread_kernel(blocks_ref, out_ref):
    for i in range(GROUP):
        out_ref[:, i * BLOCK : (i + 1) * BLOCK] = blocks_ref[i]


def spread(blocks):
    return pl.pallas_call(
        spread_kernel,
        in_specs=[IN_VMEM],
        out_specs=IN_VMEM,
        out_shape=vmem(R, COLS),
        compiler_params=PARAMS,
        cost_estimate=cost(0, 2 << 20),
    )(blocks)


def tail_kernel(other, core_ref, ortho_ref, q_ref, merged_ref, *refs):
    error_hbm, q_hbm, ortho_hbm, errors, sems, out_sems = refs[-6:]
    which = 1 - core_ref[0] if other else core_ref[0]
    outward = start([(q_ref, q_hbm.at[which]), (ortho_ref, ortho_hbm.at[which])], sems)
    rounded_p = ortho_ref[...].astype(jnp.bfloat16)
    for j in range(CHUNKS):
        approx = lax.dot_general(
            rounded_p,
            q_ref[:, chunk(j)].astype(jnp.bfloat16),
            (((0,), (0,)), ((), ())),
            preferred_element_type=jnp.float32,
        )
        error = merged_ref[:, chunk(j)].astype(jnp.float32) - approx
        errors[:, chunk(j)] = error.astype(jnp.bfloat16)
        outward += start([(errors.at[:, chunk(j)], error_hbm.at[0, which, :, chunk(j)])], out_sems.at[j])
    finish(outward)


def tail(core, ortho, q, merged, before=()):
    return pl.pallas_call(
        functools.partial(tail_kernel, bool(before)),
        in_specs=[IN_SMEM, IN_VMEM, IN_VMEM, IN_VMEM] + [IN_HBM] * len(before),
        out_specs=[IN_HBM, IN_HBM, IN_HBM],
        out_shape=(hbm(1, MATS, ROWS, COLS, dtype=jnp.bfloat16), hbm(MATS, R, COLS), hbm(MATS, R, ROWS)),
        input_output_aliases={4: 0, 5: 1, 6: 2} if before else {},
        scratch_shapes=[
            pltpu.VMEM((ROWS, COLS), jnp.bfloat16),
            pltpu.SemaphoreType.DMA((2,)),
            pltpu.SemaphoreType.DMA((CHUNKS, 1)),
        ],
        compiler_params=PARAMS,
        cost_estimate=cost(2 * ROWS * R * COLS, 4 << 20),
    )(core, keep(ortho, pltpu.VMEM), keep(q, pltpu.VMEM), keep(merged, pltpu.VMEM), *before)


def local(grads, errors, q_init):
    core = lax.axis_index("c").astype(jnp.int32)
    own = core.reshape(1)

    merged, merged_other, send, mine, theirs = left(own, grads, errors, q_init.transpose(0, 2, 1))
    terms = jnp.concatenate([mine, swap(theirs)], axis=1)
    terms, send = lax.optimization_barrier((terms, send))
    parts = [terms] + shifts(terms, "x", NX)
    received = swap(send)
    terms = sum_four(parts)
    terms = terms + shifts(terms, "w", NW)[0]
    summed = sum_four([terms] + shifts(terms, "v", NV))

    gram = jnp.einsum("kr,lr->kl", summed, summed, precision=HIGH)
    grams = [gram] + shifts(gram, "y", NY)

    half = exchange(right(summed, merged, received), ("x", "w", "y"))
    part = sum_parts(half, after=grams)
    inverse, ortho, ortho_theirs = factors(grams, summed)
    parts = [part] + shifts(part, "v", NV)

    q_own = spread(exchange(middle(parts, inverse), ("x", "w", "y")))
    q_other = swap(q_own)
    first = tail(own, ortho, q_own, merged)
    ortho_other, first = lax.optimization_barrier((swap(ortho_theirs), first))
    error_new, q_t, orthonormal = tail(own, ortho_other, q_other, merged_other, first)
    return (error_new, q_t.transpose(0, 2, 1), orthonormal.transpose(0, 2, 1))


def solution(mesh):
    fine = Mesh(mesh.devices.reshape(NX, NV, NW, NY, NC), ("x", "v", "w", "y", "c"))
    big = P(("x", "v", "w"), None, ("y", "c"), None)
    return jax.shard_map(
        local,
        mesh=fine,
        in_specs=(big, big, P()),
        out_specs=(big, P(), P(None, ("y", "c"), None)),
        check_vma=False,
    )
```

```python
import functools

import jax
import jax.numpy as jnp
from jax import lax
from jax.experimental import pallas as pl
from jax.experimental.pallas import tpu as pltpu
from jax.sharding import Mesh
from jax.sharding import PartitionSpec as P

NX, NV, NW, NY, NC = 4, 4, 2, 4, 2
COLS, R, MATS, ROWS = 8192, 32, 2, 64
DP = NX * NV * NW
GROUP = NX * NW * NY
BLOCK = COLS // GROUP
CHUNKS = 8
SPAN = COLS // CHUNKS
PER = GROUP // CHUNKS
AHEAD = 8
HIGH = lax.Precision.HIGHEST

IN_VMEM = pl.BlockSpec(memory_space=pltpu.VMEM)
IN_SMEM = pl.BlockSpec(memory_space=pltpu.SMEM)
IN_HBM = pl.BlockSpec(memory_space=pltpu.HBM)
ANYWHERE = pl.BlockSpec(memory_space=pl.ANY)
PARAMS = pltpu.CompilerParams(vmem_limit_bytes=16 * 1024 * 1024)


def cost(flops, nbytes):
    return pl.CostEstimate(flops=flops, bytes_accessed=nbytes, transcendentals=0)


def f32(*shape):
    return jax.ShapeDtypeStruct(shape, jnp.float32)


def vmem(*shape, dtype=jnp.float32):
    return pltpu.VMEM(shape, dtype)


def hbm(*shape, dtype=jnp.float32):
    return pltpu.HBM(shape, dtype)


def keep(a, space):
    return pltpu.with_memory_space_constraint(a, space)


def swap(a):
    return lax.ppermute(a, "c", [(0, 1), (1, 0)])


def shifts(a, axis, size):
    return [lax.ppermute(a, axis, [(i, (i + s) % size) for i in range(size)]) for s in (1, 3, 2)[: size - 1]]


def exchange(a, axes):
    return lax.all_to_all(a, axes, 0, 0)


def chunk(j):
    return pl.ds(j * SPAN, SPAN)


def split3(value):
    high = value.astype(jnp.bfloat16)
    rest = value - high.astype(jnp.float32)
    middle = rest.astype(jnp.bfloat16)
    low = (rest - middle.astype(jnp.float32)).astype(jnp.bfloat16)
    return high, middle, low


def start(pairs, sems):
    copies = [pltpu.make_async_copy(src, dst, sems.at[i]) for i, (src, dst) in enumerate(pairs)]
    for copy in copies:
        copy.start()
    return copies


def finish(copies):
    for copy in copies:
        copy.wait()


def left_kernel(
    core_ref, grads_hbm, errors_hbm, q_hbm, own_ref, other_ref, send_ref, mine_ref, theirs_ref, grads, errors, q, in_sems
):
    core = core_ref[0]
    inward = [
        start(
            [
                (grads_hbm.at[0, :, :, chunk(j)], grads.at[:, :, chunk(j)]),
                (errors_hbm.at[0, :, :, chunk(j)], errors.at[:, :, chunk(j)]),
                (q_hbm.at[:, :, chunk(j)], q.at[:, :, chunk(j)]),
            ],
            in_sems.at[j],
        )
        for j in range(CHUNKS)
    ]
    totals = [jnp.zeros((R, ROWS), jnp.float32) for _ in range(MATS)]
    for j in range(CHUNKS):
        finish(inward[j])
        for i, m in enumerate((core, 1 - core)):
            total = grads[m, :, chunk(j)].astype(jnp.float32) + errors[m, :, chunk(j)].astype(jnp.float32)
            merged = total.astype(jnp.bfloat16)
            totals[i] += lax.dot_general(
                q[m, :, chunk(j)], merged, (((1,), (1,)), ((), ())), preferred_element_type=jnp.float32
            )
            if i == 0:
                own_ref[:, chunk(j)] = merged
            else:
                other_ref[:, chunk(j)] = merged
                send_ref[:, chunk(j)] = merged.astype(jnp.float32)
    mine_ref[...] = totals[0]
    theirs_ref[...] = totals[1]


def left(core, grads, errors, q_t):
    return pl.pallas_call(
        left_kernel,
        in_specs=[IN_SMEM, IN_HBM, IN_HBM, IN_HBM],
        out_specs=[IN_VMEM] * 5,
        out_shape=(
            vmem(ROWS, COLS, dtype=jnp.bfloat16),
            vmem(ROWS, COLS, dtype=jnp.bfloat16),
            vmem(ROWS, COLS),
            vmem(R, ROWS),
            vmem(R, ROWS),
        ),
        scratch_shapes=[
            pltpu.VMEM((MATS, ROWS, COLS), jnp.bfloat16),
            pltpu.VMEM((MATS, ROWS, COLS), jnp.bfloat16),
            pltpu.VMEM((MATS, R, COLS), jnp.bfloat16),
            pltpu.SemaphoreType.DMA((CHUNKS, 3)),
        ],
        compiler_params=PARAMS,
        cost_estimate=cost(1 << 27, 9 << 20),
    )(core, keep(grads, pltpu.HBM), keep(errors, pltpu.HBM), keep(q_t, pltpu.HBM))


def added(parts_ref):
    value = parts_ref[0]
    for part in range(1, parts_ref.shape[0]):
        value = value + parts_ref[part]
    return value


def sum_kernel(parts_ref, *refs):
    out_ref = refs[-1]
    value = added(parts_ref)
    if len(out_ref.shape) == len(value.shape):
        out_ref[...] = value
    else:
        for copy in range(out_ref.shape[0]):
            out_ref[copy] = value


def sum_parts(parts, count=None, after=()):
    shape = parts.shape[1:] if count is None else (count,) + parts.shape[1:]
    return pl.pallas_call(
        sum_kernel,
        in_specs=[IN_VMEM] + [IN_VMEM] * len(after),
        out_specs=IN_VMEM,
        out_shape=f32(*shape),
        compiler_params=PARAMS,
        cost_estimate=cost(1 << 18, 2 << 20),
    )(parts, *[keep(a, pltpu.VMEM) for a in after])


def four_kernel(first_ref, second_ref, third_ref, fourth_ref, out_ref):
    value = (first_ref[...] + second_ref[...]) + (third_ref[...] + fourth_ref[...])
    if len(out_ref.shape) == len(value.shape):
        out_ref[...] = value
    else:
        for copy in range(out_ref.shape[0]):
            out_ref[copy] = value


def sum_four(parts, count=None):
    shape = parts[0].shape if count is None else (count,) + parts[0].shape
    return pl.pallas_call(
        four_kernel,
        in_specs=[IN_VMEM] * 4,
        out_specs=IN_VMEM,
        out_shape=f32(*shape),
        compiler_params=PARAMS,
        cost_estimate=cost(1 << 18, 2 << 20),
    )(*parts)


def middle_kernel(first_ref, second_ref, third_ref, fourth_ref, inverse_ref, out_ref):
    total = (first_ref[...] + second_ref[...]) + (third_ref[...] + fourth_ref[...])
    q = jnp.dot(inverse_ref[...], total, precision=HIGH, preferred_element_type=jnp.float32) * (1.0 / DP)
    for copy in range(GROUP):
        out_ref[copy] = q


def middle(parts, inverse):
    return pl.pallas_call(
        middle_kernel,
        in_specs=[IN_VMEM] * (NV + 1),
        out_specs=IN_VMEM,
        out_shape=vmem(GROUP, R, BLOCK),
        compiler_params=PARAMS,
        cost_estimate=cost(1 << 20, 2 << 20),
    )(*parts, inverse)


def right_kernel(summed_ref, merged_ref, received_ref, out_ref, terms, out_sems):
    pieces = jnp.concatenate(split3(summed_ref[...]), axis=0)
    outward = []
    for j in range(CHUNKS):
        both = jnp.concatenate(
            [merged_ref[:, chunk(j)], received_ref[:, chunk(j)].astype(jnp.bfloat16)], axis=0
        )
        products = jnp.dot(pieces, both, preferred_element_type=jnp.float32)
        value = products[:R] + (products[R : 2 * R] + products[2 * R :])
        for i in range(PER):
            terms[j * PER + i] = value[:, i * BLOCK : (i + 1) * BLOCK]
        outward += start([(terms.at[pl.ds(j * PER, PER)], out_ref.at[pl.ds(j * PER, PER)])], out_sems.at[j])
    finish(outward)


def right(summed, merged, received):
    return pl.pallas_call(
        right_kernel,
        in_specs=[IN_VMEM, IN_VMEM, IN_VMEM],
        out_specs=IN_HBM,
        out_shape=hbm(GROUP, R, BLOCK),
        scratch_shapes=[pltpu.VMEM((GROUP, R, BLOCK), jnp.float32), pltpu.SemaphoreType.DMA((CHUNKS, 1))],
        compiler_params=PARAMS,
        cost_estimate=cost(12 * ROWS * R * COLS, 4 << 20),
    )(summed, keep(merged, pltpu.VMEM), received)


def factor_kernel(first_ref, second_ref, third_ref, fourth_ref, summed_ref, inverse_ref, own_ref, theirs_ref):
    gram = (first_ref[...] + second_ref[...]) + (third_ref[...] + fourth_ref[...])
    row = lax.broadcasted_iota(jnp.int32, (R, 2 * R), 0)
    lane = lax.broadcasted_iota(jnp.int32, (R, 2 * R), 1)
    unit = (lane - R == row).astype(jnp.float32)[:, R:]
    x = jnp.concatenate([gram, unit], axis=1)
    for j in range(0, R, 2):
        row_a, row_b = x[j : j + 1], x[j + 1 : j + 2]
        column_a, column_b = x[:, j : j + 1], x[:, j + 1 : j + 2]
        pivot, between = row_a[:, j : j + 1], row_b[:, j : j + 1]
        inverse_a = 1.0 / pivot
        factor = between * inverse_a
        inverse_b = 1.0 / (row_b[:, j + 1 : j + 2] - factor * between)
        row_b = row_b - factor * row_a
        column_b = column_b - column_a * factor
        x = x - jnp.where(row > j, column_a * inverse_a, 0.0) * row_a
        x = x - jnp.where(row > j + 1, column_b * inverse_b, 0.0) * row_b
    diagonal = jnp.sum(jnp.where(row == lane, x, 0.0), axis=1, keepdims=True)
    inverse = x[:, R:] / jnp.sqrt(diagonal)
    inverse_ref[...] = inverse
    ortho = jnp.dot(inverse, summed_ref[...], precision=HIGH, preferred_element_type=jnp.float32)
    own_ref[...] = ortho[:, :ROWS]
    theirs_ref[...] = ortho[:, ROWS:]


def factors(grams, summed):
    return pl.pallas_call(
        factor_kernel,
        in_specs=[IN_VMEM] * (NY + 1),
        out_specs=[IN_VMEM] * 3,
        compiler_params=PARAMS,
        out_shape=(vmem(R, R), vmem(R, ROWS), vmem(R, ROWS)),
        cost_estimate=cost(1 << 20, 12 << 20),
    )(*[keep(a, pltpu.VMEM) for a in grams], keep(summed, pltpu.VMEM))


def spread_kernel(blocks_ref, out_ref):
    for i in range(GROUP):
        out_ref[:, i * BLOCK : (i + 1) * BLOCK] = blocks_ref[i]


def spread(blocks):
    return pl.pallas_call(
        spread_kernel,
        in_specs=[IN_VMEM],
        out_specs=IN_VMEM,
        out_shape=vmem(R, COLS),
        compiler_params=PARAMS,
        cost_estimate=cost(0, 2 << 20),
    )(blocks)


def tail_kernel(other, core_ref, ortho_ref, q_ref, merged_ref, *refs):
    error_hbm, q_hbm, ortho_hbm, errors, sems, out_sems = refs[-6:]
    which = 1 - core_ref[0] if other else core_ref[0]
    outward = start([(q_ref, q_hbm.at[which]), (ortho_ref, ortho_hbm.at[which])], sems)
    rounded_p = ortho_ref[...].astype(jnp.bfloat16)
    for j in range(CHUNKS):
        approx = lax.dot_general(
            rounded_p,
            q_ref[:, chunk(j)].astype(jnp.bfloat16),
            (((0,), (0,)), ((), ())),
            preferred_element_type=jnp.float32,
        )
        error = merged_ref[:, chunk(j)].astype(jnp.float32) - approx
        errors[:, chunk(j)] = error.astype(jnp.bfloat16)
        outward += start([(errors.at[:, chunk(j)], error_hbm.at[0, which, :, chunk(j)])], out_sems.at[j])
    finish(outward)


def tail(core, ortho, q, merged, before=()):
    return pl.pallas_call(
        functools.partial(tail_kernel, bool(before)),
        in_specs=[IN_SMEM, IN_VMEM, IN_VMEM, IN_VMEM] + [IN_HBM] * len(before),
        out_specs=[IN_HBM, IN_HBM, IN_HBM],
        out_shape=(hbm(1, MATS, ROWS, COLS, dtype=jnp.bfloat16), hbm(MATS, R, COLS), hbm(MATS, R, ROWS)),
        input_output_aliases={4: 0, 5: 1, 6: 2} if before else {},
        scratch_shapes=[
            pltpu.VMEM((ROWS, COLS), jnp.bfloat16),
            pltpu.SemaphoreType.DMA((2,)),
            pltpu.SemaphoreType.DMA((CHUNKS, 1)),
        ],
        compiler_params=PARAMS,
        cost_estimate=cost(2 * ROWS * R * COLS, 4 << 20),
    )(core, keep(ortho, pltpu.VMEM), keep(q, pltpu.VMEM), keep(merged, pltpu.VMEM), *before)


def local(grads, errors, q_init):
    core = lax.axis_index("c").astype(jnp.int32)
    own = core.reshape(1)

    merged, merged_other, send, mine, theirs = left(own, grads, errors, q_init.transpose(0, 2, 1))
    terms = jnp.concatenate([mine, swap(theirs)], axis=1)
    terms, send = lax.optimization_barrier((terms, send))
    parts = [terms] + shifts(terms, "x", NX)
    received = swap(send)
    terms = sum_four(parts, NV * NW)
    summed = sum_parts(exchange(terms, ("v", "w")))

    gram = jnp.einsum("kr,lr->kl", summed, summed, precision=HIGH)
    grams = [gram] + shifts(gram, "y", NY)

    half = exchange(right(summed, merged, received), ("x", "w", "y"))
    part = sum_parts(half, after=grams)
    inverse, ortho, ortho_theirs = factors(grams, summed)
    parts = [part] + shifts(part, "v", NV)

    q_own = spread(exchange(middle(parts, inverse), ("x", "w", "y")))
    q_other = swap(q_own)
    first = tail(own, ortho, q_own, merged)
    ortho_other, first = lax.optimization_barrier((swap(ortho_theirs), first))
    error_new, q_t, orthonormal = tail(own, ortho_other, q_other, merged_other, first)
    return (error_new, q_t.transpose(0, 2, 1), orthonormal.transpose(0, 2, 1))


def solution(mesh):
    fine = Mesh(mesh.devices.reshape(NX, NV, NW, NY, NC), ("x", "v", "w", "y", "c"))
    big = P(("x", "v", "w"), None, ("y", "c"), None)
    return jax.shard_map(
        local,
        mesh=fine,
        in_specs=(big, big, P()),
        out_specs=(big, P(), P(None, ("y", "c"), None)),
        check_vma=False,
    )
```

```python
import functools

import jax
import jax.numpy as jnp
from jax import lax
from jax.experimental import pallas as pl
from jax.experimental.pallas import tpu as pltpu
from jax.sharding import Mesh
from jax.sharding import PartitionSpec as P

NX, NV, NW, NY, NC = 4, 4, 2, 4, 2
COLS, R, MATS, ROWS = 8192, 32, 2, 64
DP = NX * NV * NW
GROUP = NX * NW * NY
BLOCK = COLS // GROUP
CHUNKS = 8
SPAN = COLS // CHUNKS
PER = GROUP // CHUNKS
AHEAD = 8
HIGH = lax.Precision.HIGHEST

IN_VMEM = pl.BlockSpec(memory_space=pltpu.VMEM)
IN_SMEM = pl.BlockSpec(memory_space=pltpu.SMEM)
IN_HBM = pl.BlockSpec(memory_space=pltpu.HBM)
ANYWHERE = pl.BlockSpec(memory_space=pl.ANY)
PARAMS = pltpu.CompilerParams(vmem_limit_bytes=16 * 1024 * 1024)


def cost(flops, nbytes):
    return pl.CostEstimate(flops=flops, bytes_accessed=nbytes, transcendentals=0)


def f32(*shape):
    return jax.ShapeDtypeStruct(shape, jnp.float32)


def vmem(*shape, dtype=jnp.float32):
    return pltpu.VMEM(shape, dtype)


def hbm(*shape, dtype=jnp.float32):
    return pltpu.HBM(shape, dtype)


def keep(a, space):
    return pltpu.with_memory_space_constraint(a, space)


def swap(a):
    return lax.ppermute(a, "c", [(0, 1), (1, 0)])


def shifts(a, axis, size):
    return [lax.ppermute(a, axis, [(i, (i + s) % size) for i in range(size)]) for s in (1, 3, 2)[: size - 1]]


def exchange(a, axes):
    return lax.all_to_all(a, axes, 0, 0)


def chunk(j):
    return pl.ds(j * SPAN, SPAN)


def split3(value):
    high = value.astype(jnp.bfloat16)
    rest = value - high.astype(jnp.float32)
    middle = rest.astype(jnp.bfloat16)
    low = (rest - middle.astype(jnp.float32)).astype(jnp.bfloat16)
    return high, middle, low


def start(pairs, sems):
    copies = [pltpu.make_async_copy(src, dst, sems.at[i]) for i, (src, dst) in enumerate(pairs)]
    for copy in copies:
        copy.start()
    return copies


def finish(copies):
    for copy in copies:
        copy.wait()


def left_kernel(
    core_ref, grads_hbm, errors_hbm, q_hbm, own_ref, other_ref, send_ref, mine_ref, theirs_ref, grads, errors, q, in_sems
):
    core = core_ref[0]
    inward = [
        start(
            [
                (grads_hbm.at[0, :, :, chunk(j)], grads.at[:, :, chunk(j)]),
                (errors_hbm.at[0, :, :, chunk(j)], errors.at[:, :, chunk(j)]),
                (q_hbm.at[:, :, chunk(j)], q.at[:, :, chunk(j)]),
            ],
            in_sems.at[j],
        )
        for j in range(CHUNKS)
    ]
    totals = [jnp.zeros((R, ROWS), jnp.float32) for _ in range(MATS)]
    for j in range(CHUNKS):
        finish(inward[j])
        for i, m in enumerate((core, 1 - core)):
            total = grads[m, :, chunk(j)].astype(jnp.float32) + errors[m, :, chunk(j)].astype(jnp.float32)
            merged = total.astype(jnp.bfloat16)
            totals[i] += lax.dot_general(
                q[m, :, chunk(j)], merged, (((1,), (1,)), ((), ())), preferred_element_type=jnp.float32
            )
            if i == 0:
                own_ref[:, chunk(j)] = merged
            else:
                other_ref[:, chunk(j)] = merged
                send_ref[:, chunk(j)] = merged.astype(jnp.float32)
    mine_ref[...] = totals[0]
    theirs_ref[...] = totals[1]


def left(core, grads, errors, q_t):
    return pl.pallas_call(
        left_kernel,
        in_specs=[IN_SMEM, IN_HBM, IN_HBM, IN_HBM],
        out_specs=[IN_VMEM] * 5,
        out_shape=(
            vmem(ROWS, COLS, dtype=jnp.bfloat16),
            vmem(ROWS, COLS, dtype=jnp.bfloat16),
            vmem(ROWS, COLS),
            vmem(R, ROWS),
            vmem(R, ROWS),
        ),
        scratch_shapes=[
            pltpu.VMEM((MATS, ROWS, COLS), jnp.bfloat16),
            pltpu.VMEM((MATS, ROWS, COLS), jnp.bfloat16),
            pltpu.VMEM((MATS, R, COLS), jnp.bfloat16),
            pltpu.SemaphoreType.DMA((CHUNKS, 3)),
        ],
        compiler_params=PARAMS,
        cost_estimate=cost(1 << 27, 9 << 20),
    )(core, keep(grads, pltpu.HBM), keep(errors, pltpu.HBM), keep(q_t, pltpu.HBM))


def added(parts_ref):
    value = parts_ref[0]
    for part in range(1, parts_ref.shape[0]):
        value = value + parts_ref[part]
    return value


def sum_kernel(parts_ref, *refs):
    out_ref = refs[-1]
    value = added(parts_ref)
    if len(out_ref.shape) == len(value.shape):
        out_ref[...] = value
    else:
        for copy in range(out_ref.shape[0]):
            out_ref[copy] = value


def sum_parts(parts, count=None, after=()):
    shape = parts.shape[1:] if count is None else (count,) + parts.shape[1:]
    return pl.pallas_call(
        sum_kernel,
        in_specs=[IN_VMEM] + [IN_VMEM] * len(after),
        out_specs=IN_VMEM,
        out_shape=f32(*shape),
        compiler_params=PARAMS,
        cost_estimate=cost(1 << 18, 2 << 20),
    )(parts, *[keep(a, pltpu.VMEM) for a in after])


def four_kernel(first_ref, second_ref, third_ref, fourth_ref, out_ref):
    value = (first_ref[...] + second_ref[...]) + (third_ref[...] + fourth_ref[...])
    if len(out_ref.shape) == len(value.shape):
        out_ref[...] = value
    else:
        for copy in range(out_ref.shape[0]):
            out_ref[copy] = value


def sum_four(parts, count=None):
    shape = parts[0].shape if count is None else (count,) + parts[0].shape
    return pl.pallas_call(
        four_kernel,
        in_specs=[IN_VMEM] * 4,
        out_specs=IN_VMEM,
        out_shape=f32(*shape),
        compiler_params=PARAMS,
        cost_estimate=cost(1 << 18, 2 << 20),
    )(*parts)


def middle_kernel(first_ref, second_ref, third_ref, fourth_ref, inverse_ref, out_ref):
    total = (first_ref[...] + second_ref[...]) + (third_ref[...] + fourth_ref[...])
    q = jnp.dot(inverse_ref[...], total, precision=HIGH, preferred_element_type=jnp.float32) * (1.0 / DP)
    for copy in range(GROUP):
        out_ref[copy] = q


def middle(parts, inverse):
    return pl.pallas_call(
        middle_kernel,
        in_specs=[IN_VMEM] * (NV + 1),
        out_specs=IN_VMEM,
        out_shape=vmem(GROUP, R, BLOCK),
        compiler_params=PARAMS,
        cost_estimate=cost(1 << 20, 2 << 20),
    )(*parts, inverse)


def right_kernel(summed_ref, merged_ref, received_ref, out_ref, terms, out_sems):
    pieces = jnp.concatenate(split3(summed_ref[...]), axis=0)
    outward = []
    for j in range(CHUNKS):
        both = jnp.concatenate(
            [merged_ref[:, chunk(j)], received_ref[:, chunk(j)].astype(jnp.bfloat16)], axis=0
        )
        products = jnp.dot(pieces, both, preferred_element_type=jnp.float32)
        value = products[:R] + (products[R : 2 * R] + products[2 * R :])
        for i in range(PER):
            terms[j * PER + i] = value[:, i * BLOCK : (i + 1) * BLOCK]
        outward += start([(terms.at[pl.ds(j * PER, PER)], out_ref.at[pl.ds(j * PER, PER)])], out_sems.at[j])
    finish(outward)


def right(summed, merged, received):
    return pl.pallas_call(
        right_kernel,
        in_specs=[IN_VMEM, IN_VMEM, IN_VMEM],
        out_specs=IN_HBM,
        out_shape=hbm(GROUP, R, BLOCK),
        scratch_shapes=[pltpu.VMEM((GROUP, R, BLOCK), jnp.float32), pltpu.SemaphoreType.DMA((CHUNKS, 1))],
        compiler_params=PARAMS,
        cost_estimate=cost(12 * ROWS * R * COLS, 4 << 20),
    )(summed, keep(merged, pltpu.VMEM), received)


def gram_kernel(summed_ref, out_ref):
    summed = summed_ref[...]
    gram = lax.dot_general(
        summed, summed, (((1,), (1,)), ((), ())), precision=HIGH, preferred_element_type=jnp.float32
    )
    out_ref[...] = jnp.concatenate([gram[i : i + 8] for i in range(0, R, 8)], axis=1)


def packed_gram(summed):
    return pl.pallas_call(
        gram_kernel,
        in_specs=[IN_VMEM],
        out_specs=IN_VMEM,
        out_shape=vmem(8, R * R // 8),
        compiler_params=PARAMS,
        cost_estimate=cost(1 << 18, 1 << 15),
    )(keep(summed, pltpu.VMEM))


def factor_kernel(first_ref, second_ref, third_ref, fourth_ref, summed_ref, inverse_ref, own_ref, theirs_ref):
    packed = (first_ref[...] + second_ref[...]) + (third_ref[...] + fourth_ref[...])
    gram = jnp.concatenate([packed[:, i * R : (i + 1) * R] for i in range(R // 8)], axis=0)
    row = lax.broadcasted_iota(jnp.int32, (R, 2 * R), 0)
    lane = lax.broadcasted_iota(jnp.int32, (R, 2 * R), 1)
    unit = (lane - R == row).astype(jnp.float32)[:, R:]
    x = jnp.concatenate([gram, unit], axis=1)
    for j in range(0, R, 2):
        row_a, row_b = x[j : j + 1], x[j + 1 : j + 2]
        column_a, column_b = x[:, j : j + 1], x[:, j + 1 : j + 2]
        pivot, between = row_a[:, j : j + 1], row_b[:, j : j + 1]
        inverse_a = 1.0 / pivot
        factor = between * inverse_a
        inverse_b = 1.0 / (row_b[:, j + 1 : j + 2] - factor * between)
        row_b = row_b - factor * row_a
        column_b = column_b - column_a * factor
        x = x - jnp.where(row > j, column_a * inverse_a, 0.0) * row_a
        x = x - jnp.where(row > j + 1, column_b * inverse_b, 0.0) * row_b
    diagonal = jnp.sum(jnp.where(row == lane, x, 0.0), axis=1, keepdims=True)
    inverse = x[:, R:] / jnp.sqrt(diagonal)
    inverse_ref[...] = inverse
    ortho = jnp.dot(inverse, summed_ref[...], precision=HIGH, preferred_element_type=jnp.float32)
    own_ref[...] = ortho[:, :ROWS]
    theirs_ref[...] = ortho[:, ROWS:]


def factors(grams, summed):
    return pl.pallas_call(
        factor_kernel,
        in_specs=[IN_VMEM] * (NY + 1),
        out_specs=[IN_VMEM] * 3,
        compiler_params=PARAMS,
        out_shape=(vmem(R, R), vmem(R, ROWS), vmem(R, ROWS)),
        cost_estimate=cost(1 << 20, 12 << 20),
    )(*[keep(a, pltpu.VMEM) for a in grams], keep(summed, pltpu.VMEM))


def spread_kernel(blocks_ref, out_ref):
    for i in range(GROUP):
        out_ref[:, i * BLOCK : (i + 1) * BLOCK] = blocks_ref[i]


def spread(blocks):
    return pl.pallas_call(
        spread_kernel,
        in_specs=[IN_VMEM],
        out_specs=IN_VMEM,
        out_shape=vmem(R, COLS),
        compiler_params=PARAMS,
        cost_estimate=cost(0, 2 << 20),
    )(blocks)


def tail_kernel(other, core_ref, ortho_ref, q_ref, merged_ref, *refs):
    error_hbm, q_hbm, ortho_hbm, errors, sems, out_sems = refs[-6:]
    which = 1 - core_ref[0] if other else core_ref[0]
    outward = start([(q_ref, q_hbm.at[which]), (ortho_ref, ortho_hbm.at[which])], sems)
    rounded_p = ortho_ref[...].astype(jnp.bfloat16)
    for j in range(CHUNKS):
        approx = lax.dot_general(
            rounded_p,
            q_ref[:, chunk(j)].astype(jnp.bfloat16),
            (((0,), (0,)), ((), ())),
            preferred_element_type=jnp.float32,
        )
        error = merged_ref[:, chunk(j)].astype(jnp.float32) - approx
        errors[:, chunk(j)] = error.astype(jnp.bfloat16)
        outward += start([(errors.at[:, chunk(j)], error_hbm.at[0, which, :, chunk(j)])], out_sems.at[j])
    finish(outward)


def tail(core, ortho, q, merged, before=()):
    return pl.pallas_call(
        functools.partial(tail_kernel, bool(before)),
        in_specs=[IN_SMEM, IN_VMEM, IN_VMEM, IN_VMEM] + [IN_HBM] * len(before),
        out_specs=[IN_HBM, IN_HBM, IN_HBM],
        out_shape=(hbm(1, MATS, ROWS, COLS, dtype=jnp.bfloat16), hbm(MATS, R, COLS), hbm(MATS, R, ROWS)),
        input_output_aliases={4: 0, 5: 1, 6: 2} if before else {},
        scratch_shapes=[
            pltpu.VMEM((ROWS, COLS), jnp.bfloat16),
            pltpu.SemaphoreType.DMA((2,)),
            pltpu.SemaphoreType.DMA((CHUNKS, 1)),
        ],
        compiler_params=PARAMS,
        cost_estimate=cost(2 * ROWS * R * COLS, 4 << 20),
    )(core, keep(ortho, pltpu.VMEM), keep(q, pltpu.VMEM), keep(merged, pltpu.VMEM), *before)


def local(grads, errors, q_init):
    core = lax.axis_index("c").astype(jnp.int32)
    own = core.reshape(1)

    merged, merged_other, send, mine, theirs = left(own, grads, errors, q_init.transpose(0, 2, 1))
    terms = jnp.concatenate([mine, swap(theirs)], axis=1)
    terms, send = lax.optimization_barrier((terms, send))
    parts = [terms] + shifts(terms, "x", NX)
    received = swap(send)
    terms = sum_four(parts, NV * NW)
    summed = sum_parts(exchange(terms, ("v", "w")))

    gram = packed_gram(summed)
    grams = [gram] + shifts(gram, "y", NY)

    half = exchange(right(summed, merged, received), ("x", "w", "y"))
    part = sum_parts(half, after=grams)
    inverse, ortho, ortho_theirs = factors(grams, summed)
    parts = [part] + shifts(part, "v", NV)

    q_own = spread(exchange(middle(parts, inverse), ("x", "w", "y")))
    q_other = swap(q_own)
    first = tail(own, ortho, q_own, merged)
    ortho_other, first = lax.optimization_barrier((swap(ortho_theirs), first))
    error_new, q_t, orthonormal = tail(own, ortho_other, q_other, merged_other, first)
    return (error_new, q_t.transpose(0, 2, 1), orthonormal.transpose(0, 2, 1))


def solution(mesh):
    fine = Mesh(mesh.devices.reshape(NX, NV, NW, NY, NC), ("x", "v", "w", "y", "c"))
    big = P(("x", "v", "w"), None, ("y", "c"), None)
    return jax.shard_map(
        local,
        mesh=fine,
        in_specs=(big, big, P()),
        out_specs=(big, P(), P(None, ("y", "c"), None)),
        check_vma=False,
    )
```

```python
import functools

import jax
import jax.numpy as jnp
from jax import lax
from jax.experimental import pallas as pl
from jax.experimental.pallas import tpu as pltpu
from jax.sharding import Mesh
from jax.sharding import PartitionSpec as P

NX, NV, NW, NY, NC = 4, 4, 2, 4, 2
COLS, R, MATS, ROWS = 8192, 32, 2, 64
DP = NX * NV * NW
GROUP = NX * NW * NY
BLOCK = COLS // GROUP
CHUNKS = 8
SPAN = COLS // CHUNKS
PER = GROUP // CHUNKS
AHEAD = 8
HIGH = lax.Precision.HIGHEST

IN_VMEM = pl.BlockSpec(memory_space=pltpu.VMEM)
IN_SMEM = pl.BlockSpec(memory_space=pltpu.SMEM)
IN_HBM = pl.BlockSpec(memory_space=pltpu.HBM)
ANYWHERE = pl.BlockSpec(memory_space=pl.ANY)
PARAMS = pltpu.CompilerParams(vmem_limit_bytes=16 * 1024 * 1024)


def cost(flops, nbytes):
    return pl.CostEstimate(flops=flops, bytes_accessed=nbytes, transcendentals=0)


def f32(*shape):
    return jax.ShapeDtypeStruct(shape, jnp.float32)


def vmem(*shape, dtype=jnp.float32):
    return pltpu.VMEM(shape, dtype)


def hbm(*shape, dtype=jnp.float32):
    return pltpu.HBM(shape, dtype)


def keep(a, space):
    return pltpu.with_memory_space_constraint(a, space)


def swap(a):
    return lax.ppermute(a, "c", [(0, 1), (1, 0)])


def shifts(a, axis, size):
    return [lax.ppermute(a, axis, [(i, (i + s) % size) for i in range(size)]) for s in (1, 3, 2)[: size - 1]]


def exchange(a, axes):
    return lax.all_to_all(a, axes, 0, 0)


def chunk(j):
    return pl.ds(j * SPAN, SPAN)


def split3(value):
    high = value.astype(jnp.bfloat16)
    rest = value - high.astype(jnp.float32)
    middle = rest.astype(jnp.bfloat16)
    low = (rest - middle.astype(jnp.float32)).astype(jnp.bfloat16)
    return high, middle, low


def start(pairs, sems):
    copies = [pltpu.make_async_copy(src, dst, sems.at[i]) for i, (src, dst) in enumerate(pairs)]
    for copy in copies:
        copy.start()
    return copies


def finish(copies):
    for copy in copies:
        copy.wait()


def left_kernel(
    core_ref, grads_hbm, errors_hbm, q_hbm, own_ref, other_ref, send_ref, mine_ref, theirs_ref, grads, errors, q, in_sems
):
    core = core_ref[0]
    inward = [
        start(
            [
                (grads_hbm.at[0, :, :, chunk(j)], grads.at[:, :, chunk(j)]),
                (errors_hbm.at[0, :, :, chunk(j)], errors.at[:, :, chunk(j)]),
                (q_hbm.at[:, :, chunk(j)], q.at[:, :, chunk(j)]),
            ],
            in_sems.at[j],
        )
        for j in range(CHUNKS)
    ]
    totals = [jnp.zeros((R, ROWS), jnp.float32) for _ in range(MATS)]
    for j in range(CHUNKS):
        finish(inward[j])
        for i, m in enumerate((core, 1 - core)):
            total = grads[m, :, chunk(j)].astype(jnp.float32) + errors[m, :, chunk(j)].astype(jnp.float32)
            merged = total.astype(jnp.bfloat16)
            totals[i] += lax.dot_general(
                q[m, :, chunk(j)], merged, (((1,), (1,)), ((), ())), preferred_element_type=jnp.float32
            )
            if i == 0:
                own_ref[:, chunk(j)] = merged
            else:
                other_ref[:, chunk(j)] = merged
                send_ref[:, chunk(j)] = merged.astype(jnp.float32)
    mine_ref[...] = totals[0]
    theirs_ref[...] = totals[1]


def left(core, grads, errors, q_t):
    return pl.pallas_call(
        left_kernel,
        in_specs=[IN_SMEM, IN_HBM, IN_HBM, IN_HBM],
        out_specs=[IN_VMEM] * 5,
        out_shape=(
            vmem(ROWS, COLS, dtype=jnp.bfloat16),
            vmem(ROWS, COLS, dtype=jnp.bfloat16),
            vmem(ROWS, COLS),
            vmem(R, ROWS),
            vmem(R, ROWS),
        ),
        scratch_shapes=[
            pltpu.VMEM((MATS, ROWS, COLS), jnp.bfloat16),
            pltpu.VMEM((MATS, ROWS, COLS), jnp.bfloat16),
            pltpu.VMEM((MATS, R, COLS), jnp.bfloat16),
            pltpu.SemaphoreType.DMA((CHUNKS, 3)),
        ],
        compiler_params=PARAMS,
        cost_estimate=cost(1 << 27, 9 << 20),
    )(core, keep(grads, pltpu.HBM), keep(errors, pltpu.HBM), keep(q_t, pltpu.HBM))


def added(parts_ref):
    value = parts_ref[0]
    for part in range(1, parts_ref.shape[0]):
        value = value + parts_ref[part]
    return value


def sum_kernel(parts_ref, *refs):
    out_ref = refs[-1]
    value = added(parts_ref)
    if len(out_ref.shape) == len(value.shape):
        out_ref[...] = value
    else:
        for copy in range(out_ref.shape[0]):
            out_ref[copy] = value


def sum_parts(parts, count=None, after=()):
    shape = parts.shape[1:] if count is None else (count,) + parts.shape[1:]
    return pl.pallas_call(
        sum_kernel,
        in_specs=[IN_VMEM] + [IN_VMEM] * len(after),
        out_specs=IN_VMEM,
        out_shape=f32(*shape),
        compiler_params=PARAMS,
        cost_estimate=cost(1 << 18, 2 << 20),
    )(parts, *[keep(a, pltpu.VMEM) for a in after])


def four_kernel(first_ref, second_ref, third_ref, fourth_ref, out_ref):
    value = (first_ref[...] + second_ref[...]) + (third_ref[...] + fourth_ref[...])
    if len(out_ref.shape) == len(value.shape):
        out_ref[...] = value
    else:
        for copy in range(out_ref.shape[0]):
            out_ref[copy] = value


def sum_four(parts, count=None):
    shape = parts[0].shape if count is None else (count,) + parts[0].shape
    return pl.pallas_call(
        four_kernel,
        in_specs=[IN_VMEM] * 4,
        out_specs=IN_VMEM,
        out_shape=f32(*shape),
        compiler_params=PARAMS,
        cost_estimate=cost(1 << 18, 2 << 20),
    )(*parts)


def middle_kernel(first_ref, second_ref, third_ref, fourth_ref, inverse_ref, out_ref):
    total = (first_ref[...] + second_ref[...]) + (third_ref[...] + fourth_ref[...])
    q = jnp.dot(inverse_ref[...], total, precision=HIGH, preferred_element_type=jnp.float32) * (1.0 / DP)
    for copy in range(GROUP):
        out_ref[copy] = q


def middle(parts, inverse):
    return pl.pallas_call(
        middle_kernel,
        in_specs=[IN_VMEM] * (NV + 1),
        out_specs=IN_VMEM,
        out_shape=vmem(GROUP, R, BLOCK),
        compiler_params=PARAMS,
        cost_estimate=cost(1 << 20, 2 << 20),
    )(*parts, inverse)


def right_kernel(summed_ref, merged_ref, received_ref, out_ref, terms, out_sems):
    pieces = jnp.concatenate(split3(summed_ref[...]), axis=0)
    outward = []
    for j in range(CHUNKS):
        both = jnp.concatenate(
            [merged_ref[:, chunk(j)], received_ref[:, chunk(j)].astype(jnp.bfloat16)], axis=0
        )
        products = jnp.dot(pieces, both, preferred_element_type=jnp.float32)
        value = products[:R] + (products[R : 2 * R] + products[2 * R :])
        for i in range(PER):
            terms[j * PER + i] = value[:, i * BLOCK : (i + 1) * BLOCK]
        outward += start([(terms.at[pl.ds(j * PER, PER)], out_ref.at[pl.ds(j * PER, PER)])], out_sems.at[j])
    finish(outward)


def right(summed, merged, received):
    return pl.pallas_call(
        right_kernel,
        in_specs=[IN_VMEM, IN_VMEM, IN_VMEM],
        out_specs=IN_HBM,
        out_shape=hbm(GROUP, R, BLOCK),
        scratch_shapes=[pltpu.VMEM((GROUP, R, BLOCK), jnp.float32), pltpu.SemaphoreType.DMA((CHUNKS, 1))],
        compiler_params=PARAMS,
        cost_estimate=cost(12 * ROWS * R * COLS, 4 << 20),
    )(summed, keep(merged, pltpu.VMEM), received)


def gram_kernel(summed_ref, out_ref):
    summed = summed_ref[...]
    gram = lax.dot_general(
        summed, summed, (((1,), (1,)), ((), ())), precision=HIGH, preferred_element_type=jnp.float32
    )
    out_ref[...] = jnp.concatenate([gram[i : i + 8] for i in range(0, R, 8)], axis=1)


def packed_gram(summed):
    return pl.pallas_call(
        gram_kernel,
        in_specs=[IN_VMEM],
        out_specs=IN_VMEM,
        out_shape=vmem(8, R * R // 8),
        compiler_params=PARAMS,
        cost_estimate=cost(1 << 18, 1 << 15),
    )(keep(summed, pltpu.VMEM))


def factor_kernel(first_ref, second_ref, third_ref, fourth_ref, summed_ref, inverse_ref, own_ref, theirs_ref):
    packed = (first_ref[...] + second_ref[...]) + (third_ref[...] + fourth_ref[...])
    gram = jnp.concatenate([packed[:, i * R : (i + 1) * R] for i in range(R // 8)], axis=0)
    row = lax.broadcasted_iota(jnp.int32, (R, 2 * R), 0)
    lane = lax.broadcasted_iota(jnp.int32, (R, 2 * R), 1)
    unit = (lane - R == row).astype(jnp.float32)[:, R:]
    x = jnp.concatenate([gram, unit], axis=1)
    for j in range(0, R, 2):
        row_a, row_b = x[j : j + 1], x[j + 1 : j + 2]
        column_a, column_b = x[:, j : j + 1], x[:, j + 1 : j + 2]
        pivot, between = row_a[:, j : j + 1], row_b[:, j : j + 1]
        inverse_a = 1.0 / pivot
        factor = between * inverse_a
        inverse_b = 1.0 / (row_b[:, j + 1 : j + 2] - factor * between)
        row_b = row_b - factor * row_a
        column_b = column_b - column_a * factor
        x = x - jnp.where(row > j, column_a * inverse_a, 0.0) * row_a
        x = x - jnp.where(row > j + 1, column_b * inverse_b, 0.0) * row_b
    diagonal = jnp.sum(jnp.where(row == lane, x, 0.0), axis=1, keepdims=True)
    inverse = x[:, R:] / jnp.sqrt(diagonal)
    inverse_ref[...] = inverse
    ortho = jnp.dot(inverse, summed_ref[...], precision=HIGH, preferred_element_type=jnp.float32)
    own_ref[...] = ortho[:, :ROWS]
    theirs_ref[...] = ortho[:, ROWS:]


def factors(grams, summed):
    return pl.pallas_call(
        factor_kernel,
        in_specs=[IN_VMEM] * (NY + 1),
        out_specs=[IN_VMEM] * 3,
        compiler_params=PARAMS,
        out_shape=(vmem(R, R), vmem(R, ROWS), vmem(R, ROWS)),
        cost_estimate=cost(1 << 20, 12 << 20),
    )(*[keep(a, pltpu.VMEM) for a in grams], keep(summed, pltpu.VMEM))


def spread_kernel(blocks_ref, out_ref):
    for i in range(GROUP):
        out_ref[:, i * BLOCK : (i + 1) * BLOCK] = blocks_ref[i]


def spread(blocks):
    return pl.pallas_call(
        spread_kernel,
        in_specs=[IN_VMEM],
        out_specs=IN_VMEM,
        out_shape=vmem(R, COLS),
        compiler_params=PARAMS,
        cost_estimate=cost(0, 2 << 20),
    )(blocks)


def tail_kernel(other, core_ref, ortho_ref, q_ref, merged_ref, *refs):
    error_hbm, q_hbm, ortho_hbm, errors, sems, out_sems = refs[-6:]
    which = 1 - core_ref[0] if other else core_ref[0]
    outward = start([(q_ref, q_hbm.at[which]), (ortho_ref, ortho_hbm.at[which])], sems)
    rounded_p = ortho_ref[...].astype(jnp.bfloat16)
    for j in range(CHUNKS):
        approx = lax.dot_general(
            rounded_p,
            q_ref[:, chunk(j)].astype(jnp.bfloat16),
            (((0,), (0,)), ((), ())),
            preferred_element_type=jnp.float32,
        )
        error = merged_ref[:, chunk(j)].astype(jnp.float32) - approx
        errors[:, chunk(j)] = error.astype(jnp.bfloat16)
        outward += start([(errors.at[:, chunk(j)], error_hbm.at[0, which, :, chunk(j)])], out_sems.at[j])
    finish(outward)


def tail(core, ortho, q, merged, before=()):
    return pl.pallas_call(
        functools.partial(tail_kernel, bool(before)),
        in_specs=[IN_SMEM, IN_VMEM, IN_VMEM, IN_VMEM] + [IN_HBM] * len(before),
        out_specs=[IN_HBM, IN_HBM, IN_HBM],
        out_shape=(hbm(1, MATS, ROWS, COLS, dtype=jnp.bfloat16), hbm(MATS, R, COLS), hbm(MATS, R, ROWS)),
        input_output_aliases={4: 0, 5: 1, 6: 2} if before else {},
        scratch_shapes=[
            pltpu.VMEM((ROWS, COLS), jnp.bfloat16),
            pltpu.SemaphoreType.DMA((2,)),
            pltpu.SemaphoreType.DMA((CHUNKS, 1)),
        ],
        compiler_params=PARAMS,
        cost_estimate=cost(2 * ROWS * R * COLS, 4 << 20),
    )(core, keep(ortho, pltpu.VMEM), keep(q, pltpu.VMEM), keep(merged, pltpu.VMEM), *before)


def local(grads, errors, q_init):
    core = lax.axis_index("c").astype(jnp.int32)
    own = core.reshape(1)

    merged, merged_other, send, mine, theirs = left(own, grads, errors, q_init.transpose(0, 2, 1))
    terms = jnp.concatenate([mine, swap(theirs)], axis=1)
    terms, send = lax.optimization_barrier((terms, send))
    parts = [terms] + shifts(terms, "x", NX)
    received = swap(send)
    terms = sum_four(parts, NV * NW)
    summed = sum_parts(exchange(terms, ("v", "w")))

    gram = packed_gram(summed)
    grams = [gram] + shifts(gram, "y", NY)

    half = exchange(right(summed, merged, received), ("w", "y", "x"))
    part = sum_parts(half, after=grams)
    inverse, ortho, ortho_theirs = factors(grams, summed)
    parts = [part] + shifts(part, "v", NV)

    q_own = spread(exchange(middle(parts, inverse), ("w", "y", "x")))
    q_other = swap(q_own)
    first = tail(own, ortho, q_own, merged)
    ortho_other, first = lax.optimization_barrier((swap(ortho_theirs), first))
    error_new, q_t, orthonormal = tail(own, ortho_other, q_other, merged_other, first)
    return (error_new, q_t.transpose(0, 2, 1), orthonormal.transpose(0, 2, 1))


def solution(mesh):
    fine = Mesh(mesh.devices.reshape(NX, NV, NW, NY, NC), ("x", "v", "w", "y", "c"))
    big = P(("x", "v", "w"), None, ("y", "c"), None)
    return jax.shard_map(
        local,
        mesh=fine,
        in_specs=(big, big, P()),
        out_specs=(big, P(), P(None, ("y", "c"), None)),
        check_vma=False,
    )
```

```python
import functools

import jax
import jax.numpy as jnp
from jax import lax
from jax.experimental import pallas as pl
from jax.experimental.pallas import tpu as pltpu
from jax.sharding import Mesh
from jax.sharding import PartitionSpec as P

NX, NV, NW, NY, NC = 4, 4, 2, 4, 2
COLS, R, MATS, ROWS = 8192, 32, 2, 64
DP = NX * NV * NW
GROUP = NX * NW * NY
BLOCK = COLS // GROUP
CHUNKS = 8
SPAN = COLS // CHUNKS
PER = GROUP // CHUNKS
AHEAD = 8
HIGH = lax.Precision.HIGHEST

IN_VMEM = pl.BlockSpec(memory_space=pltpu.VMEM)
IN_SMEM = pl.BlockSpec(memory_space=pltpu.SMEM)
IN_HBM = pl.BlockSpec(memory_space=pltpu.HBM)
ANYWHERE = pl.BlockSpec(memory_space=pl.ANY)
PARAMS = pltpu.CompilerParams(vmem_limit_bytes=16 * 1024 * 1024)


def cost(flops, nbytes):
    return pl.CostEstimate(flops=flops, bytes_accessed=nbytes, transcendentals=0)


def f32(*shape):
    return jax.ShapeDtypeStruct(shape, jnp.float32)


def vmem(*shape, dtype=jnp.float32):
    return pltpu.VMEM(shape, dtype)


def hbm(*shape, dtype=jnp.float32):
    return pltpu.HBM(shape, dtype)


def keep(a, space):
    return pltpu.with_memory_space_constraint(a, space)


def swap(a):
    return lax.ppermute(a, "c", [(0, 1), (1, 0)])


def shifts(a, axis, size, order=(1, 3, 2)):
    return [lax.ppermute(a, axis, [(i, (i + s) % size) for i in range(size)]) for s in order[: size - 1]]


def exchange(a, axes):
    return lax.all_to_all(a, axes, 0, 0)


def chunk(j):
    return pl.ds(j * SPAN, SPAN)


def split3(value):
    high = value.astype(jnp.bfloat16)
    rest = value - high.astype(jnp.float32)
    middle = rest.astype(jnp.bfloat16)
    low = (rest - middle.astype(jnp.float32)).astype(jnp.bfloat16)
    return high, middle, low


def start(pairs, sems):
    copies = [pltpu.make_async_copy(src, dst, sems.at[i]) for i, (src, dst) in enumerate(pairs)]
    for copy in copies:
        copy.start()
    return copies


def finish(copies):
    for copy in copies:
        copy.wait()


def left_kernel(
    core_ref, grads_hbm, errors_hbm, q_hbm, own_ref, other_ref, send_ref, mine_ref, theirs_ref, grads, errors, q, in_sems
):
    core = core_ref[0]
    inward = [
        start(
            [
                (grads_hbm.at[0, :, :, chunk(j)], grads.at[:, :, chunk(j)]),
                (errors_hbm.at[0, :, :, chunk(j)], errors.at[:, :, chunk(j)]),
                (q_hbm.at[:, :, chunk(j)], q.at[:, :, chunk(j)]),
            ],
            in_sems.at[j],
        )
        for j in range(CHUNKS)
    ]
    totals = [jnp.zeros((R, ROWS), jnp.float32) for _ in range(MATS)]
    for j in range(CHUNKS):
        finish(inward[j])
        for i, m in enumerate((core, 1 - core)):
            total = grads[m, :, chunk(j)].astype(jnp.float32) + errors[m, :, chunk(j)].astype(jnp.float32)
            merged = total.astype(jnp.bfloat16)
            totals[i] += lax.dot_general(
                q[m, :, chunk(j)], merged, (((1,), (1,)), ((), ())), preferred_element_type=jnp.float32
            )
            if i == 0:
                own_ref[:, chunk(j)] = merged
            else:
                other_ref[:, chunk(j)] = merged
                send_ref[:, chunk(j)] = merged.astype(jnp.float32)
    mine_ref[...] = totals[0]
    theirs_ref[...] = totals[1]


def left(core, grads, errors, q_t):
    return pl.pallas_call(
        left_kernel,
        in_specs=[IN_SMEM, IN_HBM, IN_HBM, IN_HBM],
        out_specs=[IN_VMEM] * 5,
        out_shape=(
            vmem(ROWS, COLS, dtype=jnp.bfloat16),
            vmem(ROWS, COLS, dtype=jnp.bfloat16),
            vmem(ROWS, COLS),
            vmem(R, ROWS),
            vmem(R, ROWS),
        ),
        scratch_shapes=[
            pltpu.VMEM((MATS, ROWS, COLS), jnp.bfloat16),
            pltpu.VMEM((MATS, ROWS, COLS), jnp.bfloat16),
            pltpu.VMEM((MATS, R, COLS), jnp.bfloat16),
            pltpu.SemaphoreType.DMA((CHUNKS, 3)),
        ],
        compiler_params=PARAMS,
        cost_estimate=cost(1 << 27, 9 << 20),
    )(core, keep(grads, pltpu.HBM), keep(errors, pltpu.HBM), keep(q_t, pltpu.HBM))


def added(parts_ref):
    value = parts_ref[0]
    for part in range(1, parts_ref.shape[0]):
        value = value + parts_ref[part]
    return value


def sum_kernel(parts_ref, *refs):
    out_ref = refs[-1]
    value = added(parts_ref)
    if len(out_ref.shape) == len(value.shape):
        out_ref[...] = value
    else:
        for copy in range(out_ref.shape[0]):
            out_ref[copy] = value


def sum_parts(parts, count=None, after=()):
    shape = parts.shape[1:] if count is None else (count,) + parts.shape[1:]
    return pl.pallas_call(
        sum_kernel,
        in_specs=[IN_VMEM] + [IN_VMEM] * len(after),
        out_specs=IN_VMEM,
        out_shape=f32(*shape),
        compiler_params=PARAMS,
        cost_estimate=cost(1 << 18, 2 << 20),
    )(parts, *[keep(a, pltpu.VMEM) for a in after])


def four_kernel(first_ref, second_ref, third_ref, fourth_ref, out_ref):
    value = (first_ref[...] + second_ref[...]) + (third_ref[...] + fourth_ref[...])
    if len(out_ref.shape) == len(value.shape):
        out_ref[...] = value
    else:
        for copy in range(out_ref.shape[0]):
            out_ref[copy] = value


def sum_four(parts, count=None):
    shape = parts[0].shape if count is None else (count,) + parts[0].shape
    return pl.pallas_call(
        four_kernel,
        in_specs=[IN_VMEM] * 4,
        out_specs=IN_VMEM,
        out_shape=f32(*shape),
        compiler_params=PARAMS,
        cost_estimate=cost(1 << 18, 2 << 20),
    )(*parts)


def middle_kernel(first_ref, second_ref, third_ref, fourth_ref, inverse_ref, out_ref):
    total = (first_ref[...] + second_ref[...]) + (third_ref[...] + fourth_ref[...])
    q = jnp.dot(inverse_ref[...], total, precision=HIGH, preferred_element_type=jnp.float32) * (1.0 / DP)
    for copy in range(GROUP):
        out_ref[copy] = q


def middle(parts, inverse):
    return pl.pallas_call(
        middle_kernel,
        in_specs=[IN_VMEM] * (NV + 1),
        out_specs=IN_VMEM,
        out_shape=vmem(GROUP, R, BLOCK),
        compiler_params=PARAMS,
        cost_estimate=cost(1 << 20, 2 << 20),
    )(*parts, inverse)


def right_kernel(summed_ref, merged_ref, received_ref, out_ref, terms, out_sems):
    pieces = jnp.concatenate(split3(summed_ref[...]), axis=0)
    outward = []
    for j in range(CHUNKS):
        both = jnp.concatenate(
            [merged_ref[:, chunk(j)], received_ref[:, chunk(j)].astype(jnp.bfloat16)], axis=0
        )
        products = jnp.dot(pieces, both, preferred_element_type=jnp.float32)
        value = products[:R] + (products[R : 2 * R] + products[2 * R :])
        for i in range(PER):
            terms[j * PER + i] = value[:, i * BLOCK : (i + 1) * BLOCK]
        outward += start([(terms.at[pl.ds(j * PER, PER)], out_ref.at[pl.ds(j * PER, PER)])], out_sems.at[j])
    finish(outward)


def right(summed, merged, received):
    return pl.pallas_call(
        right_kernel,
        in_specs=[IN_VMEM, IN_VMEM, IN_VMEM],
        out_specs=IN_HBM,
        out_shape=hbm(GROUP, R, BLOCK),
        scratch_shapes=[pltpu.VMEM((GROUP, R, BLOCK), jnp.float32), pltpu.SemaphoreType.DMA((CHUNKS, 1))],
        compiler_params=PARAMS,
        cost_estimate=cost(12 * ROWS * R * COLS, 4 << 20),
    )(summed, keep(merged, pltpu.VMEM), received)


def gram_kernel(summed_ref, out_ref):
    summed = summed_ref[...]
    gram = lax.dot_general(
        summed, summed, (((1,), (1,)), ((), ())), precision=HIGH, preferred_element_type=jnp.float32
    )
    out_ref[...] = jnp.concatenate([gram[i : i + 8] for i in range(0, R, 8)], axis=1)


def packed_gram(summed):
    return pl.pallas_call(
        gram_kernel,
        in_specs=[IN_VMEM],
        out_specs=IN_VMEM,
        out_shape=vmem(8, R * R // 8),
        compiler_params=PARAMS,
        cost_estimate=cost(1 << 18, 1 << 15),
    )(keep(summed, pltpu.VMEM))


def factor_kernel(first_ref, second_ref, third_ref, fourth_ref, summed_ref, inverse_ref, own_ref, theirs_ref):
    packed = (first_ref[...] + second_ref[...]) + (third_ref[...] + fourth_ref[...])
    gram = jnp.concatenate([packed[:, i * R : (i + 1) * R] for i in range(R // 8)], axis=0)
    row = lax.broadcasted_iota(jnp.int32, (R, 2 * R), 0)
    lane = lax.broadcasted_iota(jnp.int32, (R, 2 * R), 1)
    unit = (lane - R == row).astype(jnp.float32)[:, R:]
    x = jnp.concatenate([gram, unit], axis=1)
    for j in range(0, R, 2):
        row_a, row_b = x[j : j + 1], x[j + 1 : j + 2]
        column_a, column_b = x[:, j : j + 1], x[:, j + 1 : j + 2]
        pivot, between = row_a[:, j : j + 1], row_b[:, j : j + 1]
        inverse_a = 1.0 / pivot
        factor = between * inverse_a
        inverse_b = 1.0 / (row_b[:, j + 1 : j + 2] - factor * between)
        row_b = row_b - factor * row_a
        column_b = column_b - column_a * factor
        x = x - jnp.where(row > j, column_a * inverse_a, 0.0) * row_a
        x = x - jnp.where(row > j + 1, column_b * inverse_b, 0.0) * row_b
    diagonal = jnp.sum(jnp.where(row == lane, x, 0.0), axis=1, keepdims=True)
    inverse = x[:, R:] / jnp.sqrt(diagonal)
    inverse_ref[...] = inverse
    ortho = jnp.dot(inverse, summed_ref[...], precision=HIGH, preferred_element_type=jnp.float32)
    own_ref[...] = ortho[:, :ROWS]
    theirs_ref[...] = ortho[:, ROWS:]


def factors(grams, summed):
    return pl.pallas_call(
        factor_kernel,
        in_specs=[IN_VMEM] * (NY + 1),
        out_specs=[IN_VMEM] * 3,
        compiler_params=PARAMS,
        out_shape=(vmem(R, R), vmem(R, ROWS), vmem(R, ROWS)),
        cost_estimate=cost(1 << 20, 12 << 20),
    )(*[keep(a, pltpu.VMEM) for a in grams], keep(summed, pltpu.VMEM))


def spread_kernel(blocks_ref, out_ref):
    for i in range(GROUP):
        out_ref[:, i * BLOCK : (i + 1) * BLOCK] = blocks_ref[i]


def spread(blocks):
    return pl.pallas_call(
        spread_kernel,
        in_specs=[IN_VMEM],
        out_specs=IN_VMEM,
        out_shape=vmem(R, COLS),
        compiler_params=PARAMS,
        cost_estimate=cost(0, 2 << 20),
    )(blocks)


def tail_kernel(other, core_ref, ortho_ref, q_ref, merged_ref, *refs):
    error_hbm, q_hbm, ortho_hbm, errors, sems, out_sems = refs[-6:]
    which = 1 - core_ref[0] if other else core_ref[0]
    outward = start([(q_ref, q_hbm.at[which]), (ortho_ref, ortho_hbm.at[which])], sems)
    rounded_p = ortho_ref[...].astype(jnp.bfloat16)
    for j in range(CHUNKS):
        approx = lax.dot_general(
            rounded_p,
            q_ref[:, chunk(j)].astype(jnp.bfloat16),
            (((0,), (0,)), ((), ())),
            preferred_element_type=jnp.float32,
        )
        error = merged_ref[:, chunk(j)].astype(jnp.float32) - approx
        errors[:, chunk(j)] = error.astype(jnp.bfloat16)
        outward += start([(errors.at[:, chunk(j)], error_hbm.at[0, which, :, chunk(j)])], out_sems.at[j])
    finish(outward)


def tail(core, ortho, q, merged, before=()):
    return pl.pallas_call(
        functools.partial(tail_kernel, bool(before)),
        in_specs=[IN_SMEM, IN_VMEM, IN_VMEM, IN_VMEM] + [IN_HBM] * len(before),
        out_specs=[IN_HBM, IN_HBM, IN_HBM],
        out_shape=(hbm(1, MATS, ROWS, COLS, dtype=jnp.bfloat16), hbm(MATS, R, COLS), hbm(MATS, R, ROWS)),
        input_output_aliases={4: 0, 5: 1, 6: 2} if before else {},
        scratch_shapes=[
            pltpu.VMEM((ROWS, COLS), jnp.bfloat16),
            pltpu.SemaphoreType.DMA((2,)),
            pltpu.SemaphoreType.DMA((CHUNKS, 1)),
        ],
        compiler_params=PARAMS,
        cost_estimate=cost(2 * ROWS * R * COLS, 4 << 20),
    )(core, keep(ortho, pltpu.VMEM), keep(q, pltpu.VMEM), keep(merged, pltpu.VMEM), *before)


def local(grads, errors, q_init):
    core = lax.axis_index("c").astype(jnp.int32)
    own = core.reshape(1)

    merged, merged_other, send, mine, theirs = left(own, grads, errors, q_init.transpose(0, 2, 1))
    terms = jnp.concatenate([mine, swap(theirs)], axis=1)
    terms, send = lax.optimization_barrier((terms, send))
    parts = [terms] + shifts(terms, "x", NX)
    received = swap(send)
    terms = sum_four(parts, NV * NW)
    summed = sum_parts(exchange(terms, ("v", "w")))

    gram = packed_gram(summed)
    grams = [gram] + shifts(gram, "y", NY)

    half = exchange(right(summed, merged, received), ("w", "y", "x"))
    part = sum_parts(half, after=grams)
    inverse, ortho, ortho_theirs = factors(grams, summed)
    parts = [part] + shifts(part, "v", NV, (3, 1, 2))

    q_own = spread(exchange(middle(parts, inverse), ("w", "y", "x")))
    q_other = swap(q_own)
    first = tail(own, ortho, q_own, merged)
    ortho_other, first = lax.optimization_barrier((swap(ortho_theirs), first))
    error_new, q_t, orthonormal = tail(own, ortho_other, q_other, merged_other, first)
    return (error_new, q_t.transpose(0, 2, 1), orthonormal.transpose(0, 2, 1))


def solution(mesh):
    fine = Mesh(mesh.devices.reshape(NX, NV, NW, NY, NC), ("x", "v", "w", "y", "c"))
    big = P(("x", "v", "w"), None, ("y", "c"), None)
    return jax.shard_map(
        local,
        mesh=fine,
        in_specs=(big, big, P()),
        out_specs=(big, P(), P(None, ("y", "c"), None)),
        check_vma=False,
    )
```

```python
import functools

import jax
import jax.numpy as jnp
from jax import lax
from jax.experimental import pallas as pl
from jax.experimental.pallas import tpu as pltpu
from jax.sharding import Mesh
from jax.sharding import PartitionSpec as P

NX, NV, NW, NY, NC = 4, 4, 2, 4, 2
COLS, R, MATS, ROWS = 8192, 32, 2, 64
DP = NX * NV * NW
GROUP = NX * NW * NY
BLOCK = COLS // GROUP
CHUNKS = 8
SPAN = COLS // CHUNKS
PER = GROUP // CHUNKS
AHEAD = 8
HIGH = lax.Precision.HIGHEST

IN_VMEM = pl.BlockSpec(memory_space=pltpu.VMEM)
IN_SMEM = pl.BlockSpec(memory_space=pltpu.SMEM)
IN_HBM = pl.BlockSpec(memory_space=pltpu.HBM)
ANYWHERE = pl.BlockSpec(memory_space=pl.ANY)
PARAMS = pltpu.CompilerParams(vmem_limit_bytes=16 * 1024 * 1024)


def cost(flops, nbytes):
    return pl.CostEstimate(flops=flops, bytes_accessed=nbytes, transcendentals=0)


def f32(*shape):
    return jax.ShapeDtypeStruct(shape, jnp.float32)


def vmem(*shape, dtype=jnp.float32):
    return pltpu.VMEM(shape, dtype)


def hbm(*shape, dtype=jnp.float32):
    return pltpu.HBM(shape, dtype)


def keep(a, space):
    return pltpu.with_memory_space_constraint(a, space)


def swap(a):
    return lax.ppermute(a, "c", [(0, 1), (1, 0)])


def shifts(a, axis, size, order=(1, 3, 2)):
    return [lax.ppermute(a, axis, [(i, (i + s) % size) for i in range(size)]) for s in order[: size - 1]]


def exchange(a, axes):
    return lax.all_to_all(a, axes, 0, 0)


def chunk(j):
    return pl.ds(j * SPAN, SPAN)


def split3(value):
    high = value.astype(jnp.bfloat16)
    rest = value - high.astype(jnp.float32)
    middle = rest.astype(jnp.bfloat16)
    low = (rest - middle.astype(jnp.float32)).astype(jnp.bfloat16)
    return high, middle, low


def start(pairs, sems):
    copies = [pltpu.make_async_copy(src, dst, sems.at[i]) for i, (src, dst) in enumerate(pairs)]
    for copy in copies:
        copy.start()
    return copies


def finish(copies):
    for copy in copies:
        copy.wait()


def left_kernel(
    core_ref, grads_hbm, errors_hbm, q_hbm, own_ref, other_ref, send_ref, mine_ref, theirs_ref, grads, errors, q, in_sems
):
    core = core_ref[0]
    inward = [
        start(
            [
                (grads_hbm.at[0, :, :, chunk(j)], grads.at[:, :, chunk(j)]),
                (errors_hbm.at[0, :, :, chunk(j)], errors.at[:, :, chunk(j)]),
                (q_hbm.at[:, :, chunk(j)], q.at[:, :, chunk(j)]),
            ],
            in_sems.at[j],
        )
        for j in range(CHUNKS)
    ]
    totals = [jnp.zeros((R, ROWS), jnp.float32) for _ in range(MATS)]
    for j in range(CHUNKS):
        finish(inward[j])
        for i, m in enumerate((core, 1 - core)):
            total = grads[m, :, chunk(j)].astype(jnp.float32) + errors[m, :, chunk(j)].astype(jnp.float32)
            merged = total.astype(jnp.bfloat16)
            totals[i] += lax.dot_general(
                q[m, :, chunk(j)], merged, (((1,), (1,)), ((), ())), preferred_element_type=jnp.float32
            )
            if i == 0:
                own_ref[:, chunk(j)] = merged
            else:
                other_ref[:, chunk(j)] = merged
                send_ref[:, chunk(j)] = merged.astype(jnp.float32)
    mine_ref[...] = totals[0]
    theirs_ref[...] = totals[1]


def left(core, grads, errors, q_t):
    return pl.pallas_call(
        left_kernel,
        in_specs=[IN_SMEM, IN_HBM, IN_HBM, IN_HBM],
        out_specs=[IN_VMEM] * 5,
        out_shape=(
            vmem(ROWS, COLS, dtype=jnp.bfloat16),
            vmem(ROWS, COLS, dtype=jnp.bfloat16),
            vmem(ROWS, COLS),
            vmem(R, ROWS),
            vmem(R, ROWS),
        ),
        scratch_shapes=[
            pltpu.VMEM((MATS, ROWS, COLS), jnp.bfloat16),
            pltpu.VMEM((MATS, ROWS, COLS), jnp.bfloat16),
            pltpu.VMEM((MATS, R, COLS), jnp.bfloat16),
            pltpu.SemaphoreType.DMA((CHUNKS, 3)),
        ],
        compiler_params=PARAMS,
        cost_estimate=cost(1 << 27, 9 << 20),
    )(core, keep(grads, pltpu.HBM), keep(errors, pltpu.HBM), keep(q_t, pltpu.HBM))


def added(parts_ref):
    value = parts_ref[0]
    for part in range(1, parts_ref.shape[0]):
        value = value + parts_ref[part]
    return value


def sum_kernel(parts_ref, *refs):
    out_ref = refs[-1]
    value = added(parts_ref)
    if len(out_ref.shape) == len(value.shape):
        out_ref[...] = value
    else:
        for copy in range(out_ref.shape[0]):
            out_ref[copy] = value


def sum_parts(parts, count=None, after=()):
    shape = parts.shape[1:] if count is None else (count,) + parts.shape[1:]
    return pl.pallas_call(
        sum_kernel,
        in_specs=[IN_VMEM] + [IN_VMEM] * len(after),
        out_specs=IN_VMEM,
        out_shape=f32(*shape),
        compiler_params=PARAMS,
        cost_estimate=cost(1 << 18, 2 << 20),
    )(parts, *[keep(a, pltpu.VMEM) for a in after])


def four_kernel(first_ref, second_ref, third_ref, fourth_ref, out_ref):
    value = (first_ref[...] + second_ref[...]) + (third_ref[...] + fourth_ref[...])
    if len(out_ref.shape) == len(value.shape):
        out_ref[...] = value
    else:
        for copy in range(out_ref.shape[0]):
            out_ref[copy] = value


def sum_four(parts, count=None):
    shape = parts[0].shape if count is None else (count,) + parts[0].shape
    return pl.pallas_call(
        four_kernel,
        in_specs=[IN_VMEM] * 4,
        out_specs=IN_VMEM,
        out_shape=f32(*shape),
        compiler_params=PARAMS,
        cost_estimate=cost(1 << 18, 2 << 20),
    )(*parts)


def middle_kernel(first_ref, second_ref, third_ref, fourth_ref, inverse_ref, out_ref):
    total = (first_ref[...] + second_ref[...]) + (third_ref[...] + fourth_ref[...])
    q = jnp.dot(inverse_ref[...], total, precision=HIGH, preferred_element_type=jnp.float32) * (1.0 / DP)
    for copy in range(GROUP):
        out_ref[copy] = q


def middle(parts, inverse):
    return pl.pallas_call(
        middle_kernel,
        in_specs=[IN_VMEM] * (NV + 1),
        out_specs=IN_VMEM,
        out_shape=vmem(GROUP, R, BLOCK),
        compiler_params=PARAMS,
        cost_estimate=cost(1 << 20, 2 << 20),
    )(*parts, inverse)


def right_kernel(summed_ref, merged_ref, received_ref, out_ref, terms, out_sems):
    pieces = jnp.concatenate(split3(summed_ref[...]), axis=0)
    outward = []
    for j in range(CHUNKS):
        both = jnp.concatenate(
            [merged_ref[:, chunk(j)], received_ref[:, chunk(j)].astype(jnp.bfloat16)], axis=0
        )
        products = jnp.dot(pieces, both, preferred_element_type=jnp.float32)
        value = products[:R] + (products[R : 2 * R] + products[2 * R :])
        for i in range(PER):
            terms[j * PER + i] = value[:, i * BLOCK : (i + 1) * BLOCK]
        outward += start([(terms.at[pl.ds(j * PER, PER)], out_ref.at[pl.ds(j * PER, PER)])], out_sems.at[j])
    finish(outward)


def right(summed, merged, received):
    return pl.pallas_call(
        right_kernel,
        in_specs=[IN_VMEM, IN_VMEM, IN_VMEM],
        out_specs=IN_HBM,
        out_shape=hbm(GROUP, R, BLOCK),
        scratch_shapes=[pltpu.VMEM((GROUP, R, BLOCK), jnp.float32), pltpu.SemaphoreType.DMA((CHUNKS, 1))],
        compiler_params=PARAMS,
        cost_estimate=cost(12 * ROWS * R * COLS, 4 << 20),
    )(summed, keep(merged, pltpu.VMEM), received)


def gram_kernel(summed_ref, out_ref):
    summed = summed_ref[...]
    gram = lax.dot_general(
        summed, summed, (((1,), (1,)), ((), ())), precision=HIGH, preferred_element_type=jnp.float32
    )
    out_ref[...] = jnp.concatenate([gram[i : i + 8] for i in range(0, R, 8)], axis=1)


def packed_gram(summed):
    return pl.pallas_call(
        gram_kernel,
        in_specs=[IN_VMEM],
        out_specs=IN_VMEM,
        out_shape=vmem(8, R * R // 8),
        compiler_params=PARAMS,
        cost_estimate=cost(1 << 18, 1 << 15),
    )(keep(summed, pltpu.VMEM))


def factor_kernel(first_ref, second_ref, third_ref, fourth_ref, summed_ref, inverse_ref, own_ref, theirs_ref):
    packed = (first_ref[...] + second_ref[...]) + (third_ref[...] + fourth_ref[...])
    gram = jnp.concatenate([packed[:, i * R : (i + 1) * R] for i in range(R // 8)], axis=0)
    row = lax.broadcasted_iota(jnp.int32, (R, 2 * R), 0)
    lane = lax.broadcasted_iota(jnp.int32, (R, 2 * R), 1)
    unit = (lane - R == row).astype(jnp.float32)[:, R:]
    x = jnp.concatenate([gram, unit], axis=1)
    for j in range(0, R, 2):
        row_a, row_b = x[j : j + 1], x[j + 1 : j + 2]
        column_a, column_b = x[:, j : j + 1], x[:, j + 1 : j + 2]
        pivot, between = row_a[:, j : j + 1], row_b[:, j : j + 1]
        inverse_a = 1.0 / pivot
        factor = between * inverse_a
        inverse_b = 1.0 / (row_b[:, j + 1 : j + 2] - factor * between)
        row_b = row_b - factor * row_a
        column_b = column_b - column_a * factor
        x = x - jnp.where(row > j, column_a * inverse_a, 0.0) * row_a
        x = x - jnp.where(row > j + 1, column_b * inverse_b, 0.0) * row_b
    diagonal = jnp.sum(jnp.where(row == lane, x, 0.0), axis=1, keepdims=True)
    inverse = x[:, R:] / jnp.sqrt(diagonal)
    inverse_ref[...] = inverse
    ortho = jnp.dot(inverse, summed_ref[...], precision=HIGH, preferred_element_type=jnp.float32)
    own_ref[...] = ortho[:, :ROWS]
    theirs_ref[...] = ortho[:, ROWS:]


def factors(grams, summed):
    return pl.pallas_call(
        factor_kernel,
        in_specs=[IN_VMEM] * (NY + 1),
        out_specs=[IN_VMEM] * 3,
        compiler_params=PARAMS,
        out_shape=(vmem(R, R), vmem(R, ROWS), vmem(R, ROWS)),
        cost_estimate=cost(1 << 20, 12 << 20),
    )(*[keep(a, pltpu.VMEM) for a in grams], keep(summed, pltpu.VMEM))


def spread_kernel(blocks_ref, out_ref):
    for i in range(GROUP):
        out_ref[:, i * BLOCK : (i + 1) * BLOCK] = blocks_ref[i]


def spread(blocks):
    return pl.pallas_call(
        spread_kernel,
        in_specs=[IN_VMEM],
        out_specs=IN_VMEM,
        out_shape=vmem(R, COLS),
        compiler_params=PARAMS,
        cost_estimate=cost(0, 2 << 20),
    )(blocks)


def tail_kernel(other, core_ref, ortho_ref, q_ref, merged_ref, *refs):
    error_hbm, q_hbm, ortho_hbm, errors, sems, out_sems = refs[-6:]
    which = 1 - core_ref[0] if other else core_ref[0]
    outward = start([(q_ref, q_hbm.at[which]), (ortho_ref, ortho_hbm.at[which])], sems)
    rounded_p = ortho_ref[...].astype(jnp.bfloat16)
    for j in range(CHUNKS):
        approx = lax.dot_general(
            rounded_p,
            q_ref[:, chunk(j)].astype(jnp.bfloat16),
            (((0,), (0,)), ((), ())),
            preferred_element_type=jnp.float32,
        )
        error = merged_ref[:, chunk(j)].astype(jnp.float32) - approx
        errors[:, chunk(j)] = error.astype(jnp.bfloat16)
        outward += start([(errors.at[:, chunk(j)], error_hbm.at[0, which, :, chunk(j)])], out_sems.at[j])
    finish(outward)


def tail(core, ortho, q, merged, before=()):
    return pl.pallas_call(
        functools.partial(tail_kernel, bool(before)),
        in_specs=[IN_SMEM, IN_VMEM, IN_VMEM, IN_VMEM] + [IN_HBM] * len(before),
        out_specs=[IN_HBM, IN_HBM, IN_HBM],
        out_shape=(hbm(1, MATS, ROWS, COLS, dtype=jnp.bfloat16), hbm(MATS, R, COLS), hbm(MATS, R, ROWS)),
        input_output_aliases={4: 0, 5: 1, 6: 2} if before else {},
        scratch_shapes=[
            pltpu.VMEM((ROWS, COLS), jnp.bfloat16),
            pltpu.SemaphoreType.DMA((2,)),
            pltpu.SemaphoreType.DMA((CHUNKS, 1)),
        ],
        compiler_params=PARAMS,
        cost_estimate=cost(2 * ROWS * R * COLS, 4 << 20),
    )(core, keep(ortho, pltpu.VMEM), keep(q, pltpu.VMEM), keep(merged, pltpu.VMEM), *before)


def local(grads, errors, q_init):
    core = lax.axis_index("c").astype(jnp.int32)
    own = core.reshape(1)

    merged, merged_other, send, mine, theirs = left(own, grads, errors, q_init.transpose(0, 2, 1))
    terms = jnp.concatenate([mine, swap(theirs)], axis=1)
    terms, send = lax.optimization_barrier((terms, send))
    parts = [terms] + shifts(terms, "x", NX)
    received = swap(send)
    terms = sum_four(parts, NV * NW)
    summed = sum_parts(exchange(terms, ("v", "w")))

    gram = packed_gram(summed)
    grams = [gram] + shifts(gram, "y", NY, (3, 1, 2))

    half = exchange(right(summed, merged, received), ("w", "y", "x"))
    part = sum_parts(half, after=grams)
    inverse, ortho, ortho_theirs = factors(grams, summed)
    parts = [part] + shifts(part, "v", NV, (3, 1, 2))

    q_own = spread(exchange(middle(parts, inverse), ("w", "y", "x")))
    q_other = swap(q_own)
    first = tail(own, ortho, q_own, merged)
    ortho_other, first = lax.optimization_barrier((swap(ortho_theirs), first))
    error_new, q_t, orthonormal = tail(own, ortho_other, q_other, merged_other, first)
    return (error_new, q_t.transpose(0, 2, 1), orthonormal.transpose(0, 2, 1))


def solution(mesh):
    fine = Mesh(mesh.devices.reshape(NX, NV, NW, NY, NC), ("x", "v", "w", "y", "c"))
    big = P(("x", "v", "w"), None, ("y", "c"), None)
    return jax.shard_map(
        local,
        mesh=fine,
        in_specs=(big, big, P()),
        out_specs=(big, P(), P(None, ("y", "c"), None)),
        check_vma=False,
    )
```
